32 devices in a mesh: section: 2 (over core), dp: 4 (over z), rep: 4 (over y, x).
Axes of the slice: x: 2, y: 2, z: 4, core: 2. Of those that a mesh axis runs over, the one named last changes fastest.
Arguments:
- inputs: bfloat16 [32768, 512], P(('dp', 'rep')), may hold values from -6 to 6
- cotangent: bfloat16 [32768, 512], P(('dp', 'rep')), may hold values from -6 to 6
- domain_ids: int32 [32], P(('dp', 'rep')), may hold values from 0 to 15
- group_of: int32 [16], replicated, may hold values from 0 to 3
- group_weights: float32 [4], replicated, may hold values from 0.25 to 4
- norm_gains: bfloat16 [2, 2, 512], P('section'), may hold values from 0.5 to 1.5
- norm_biases: bfloat16 [2, 2, 512], P('section'), may hold values from -1.1953125 to 1.1953125
- w_in: bfloat16 [2, 512, 2048], P('section'), may hold values from -0.25 to 0.25
- w_out: bfloat16 [2, 512, 512], P('section'), may hold values from -1 to 1
- w_up: bfloat16 [2, 512, 2048], P('section'), may hold values from -0.25 to 0.25
- in_bias: bfloat16 [2, 2048], P('section'), may hold values from -1.1953125 to 1.1953125
- w_down: bfloat16 [2, 2048, 512], P('section'), may hold values from -0.125 to 0.125
- out_bias: bfloat16 [2, 512], P('section'), may hold values from -1.1953125 to 1.1953125
Outputs:
- layer_outputs: float32 [2, 32768, 512], P('section', ('dp', 'rep'))
- input_grads: float32 [2, 32768, 512], P('section', ('dp', 'rep'))
- g_norm_gains: float32 [2, 2, 512], P('section')
- g_norm_biases: float32 [2, 2, 512], P('section')
- g_w_in: float32 [2, 512, 2048], P('section')
- g_w_out: float32 [2, 512, 512], P('section')
- g_w_up: float32 [2, 512, 2048], P('section')
- g_in_bias: float32 [2, 2048], P('section')
- g_w_down: float32 [2, 2048, 512], P('section')
- g_out_bias: float32 [2, 512], P('section')
- slot_mass: float32 [64], replicated
The draws below stay inside these ranges and needn't reach their ends.
All inputs are finite; a program needn't handle non-finite values.
Results may differ from the reference program's by a relative error of at most 0.013.
The reference program's roundings to bfloat16 on the way count: a program that leaves them out, or rounds other values in their place, can miss the bound.
Values may be sent and summed in bfloat16 or wider, within the bound.
No kernel may reach another device: no remote copies, remote signals or barrier semaphores. Data moves between devices by JAX's collectives and lax.ppermute only.
A program may use at most 576 MiB of HBM per device.

```python
import math
import jax
import jax.numpy as jnp
from jax import lax

D = 512
HEADS = 8
DH = 64
SLOTS = 64
FF = 2048
BLOCK = 512
MB = 2
LEN = 1024
DOMAINS = 16
GROUPS = 4
SEQS = 32
TOKENS = 32768


def with_ends(entries, key, least, largest):
    shape = entries.shape
    place = [jax.random.randint(jax.random.fold_in(key, axis), (), 0, shape[axis]) for axis in range(len(shape))]
    entries = entries.at[tuple(place)].set(least)
    longest = shape.index(max(shape))
    place[longest] = (place[longest] + 1) % shape[longest]
    return entries.at[tuple(place)].set(largest)


def steps_of(key, shape, pieces, least, largest):
    gain, own = 1.0, jax.random.fold_in(key, 6)
    for position, blocks in pieces:
        heights = jnp.exp(jax.random.uniform(jax.random.fold_in(own, position), (blocks,), jnp.float32, least / len(pieces), largest / len(pieces)))
        gain = gain * jnp.repeat(heights, shape[position] // blocks).reshape([-1 if axis == position else 1 for axis in range(len(shape))])
    return gain


def scatter_about(own_key, dims, deviation, bound, split=(), kind=jnp.bfloat16):
    factor_of = steps_of(own_key, dims, split, -0.22, 0.18) if split else 1.0
    drawn = jax.random.normal(own_key, dims, jnp.float32) * deviation * factor_of
    return jnp.minimum(jnp.maximum(drawn, -bound), bound).astype(kind)


def setup_inputs(seed: int = 0) -> dict:
    key_list = jax.random.split(jax.random.key(seed), 14)
    inputs = scatter_about(key_list[0], (TOKENS, D), 1.0, 6.0, ((0, 16),))
    cotangent = scatter_about(key_list[1], (TOKENS, D), 1.0, 6.0, ((0, 16),))
    domain_ids = with_ends(jax.random.randint(key_list[2], (SEQS,), 0, DOMAINS), jax.random.fold_in(key_list[2], 1), 0, DOMAINS - 1).astype(jnp.int32)
    group_of = with_ends(jax.random.randint(key_list[3], (DOMAINS,), 0, GROUPS), jax.random.fold_in(key_list[3], 1), 0, GROUPS - 1).astype(jnp.int32)
    group_weights = jnp.clip(jnp.exp(jax.random.uniform(key_list[4], (GROUPS,), jnp.float32, math.log(0.25), math.log(4.0))), 0.25, 4.0)
    norm_gains = jnp.clip(1.0 + 0.1 * jax.random.normal(key_list[5], (2, 2, D), jnp.float32), 0.5, 1.5).astype(jnp.bfloat16)
    norm_biases = scatter_about(key_list[6], (2, 2, D), 0.2, 1.1953125, ((0, 2),))
    w_in = scatter_about(key_list[7], (2, D, 3 * HEADS * DH + HEADS * SLOTS), D ** -0.5, 0.25, ((0, 2),))
    w_out = scatter_about(key_list[8], (2, HEADS * DH, D), (HEADS * DH // 16) ** -0.5, 1.0, ((0, 2),))
    w_up = scatter_about(key_list[9], (2, D, FF), D ** -0.5, 0.25, ((0, 2),))
    in_bias = scatter_about(key_list[10], (2, FF), 0.2, 1.1953125, ((0, 2),))
    w_down = scatter_about(key_list[11], (2, FF, D), FF ** -0.5, 0.125, ((0, 2),))
    out_bias = scatter_about(key_list[12], (2, D), 0.2, 1.1953125, ((0, 2),))
    return dict(inputs=inputs, cotangent=cotangent, domain_ids=domain_ids, group_of=group_of, group_weights=group_weights, norm_gains=norm_gains, norm_biases=norm_biases, w_in=w_in, w_out=w_out, w_up=w_up, in_bias=in_bias, w_down=w_down, out_bias=out_bias)


EPSILON = 1e-05
running_peak_logit = lax.Precision.HIGHEST

@jax.custom_vjp
def low(v):
    return lax.optimization_barrier(v.astype(jnp.bfloat16)).astype(jnp.float32)

@jax.custom_vjp
def low_back(v):
    return v

def low_keep(v):
    return (low(v), None)

def low_pass(kept, grad):
    return (grad,)

def back_keep(v):
    return (v, None)

def back_low(kept, grad):
    return (low(grad),)
low.defvjp(low_keep, low_pass)
low_back.defvjp(back_keep, back_low)

def project(left_side, right_side):
    return jnp.dot(left_side, right_side, precision=running_peak_logit)

def normalize(hidden, gain_row, bias_row):
    center = hidden - lax.optimization_barrier(jnp.mean(hidden, axis=-1, keepdims=True))
    spread = lax.optimization_barrier(jnp.mean(center * center, axis=-1, keepdims=True))
    return center * lax.rsqrt(spread + EPSILON) * gain_row + bias_row

def slot_block(state_in, segment):
    slot_key_state, slot_value_state, mass_state = state_in
    query_matrix, key_matrix, value_matrix, logits = segment
    softmax_probabilities = jnp.exp(logits)
    extent = softmax_probabilities.shape[0]
    causal = (jnp.arange(extent)[:, None] >= jnp.arange(extent)[None, :]).astype(jnp.float32)
    running_totals = jnp.einsum('ti,ihm->thm', causal, softmax_probabilities, precision=running_peak_logit) + mass_state[None]
    affinity = jnp.einsum('thd,ihd->hti', query_matrix, key_matrix, precision=running_peak_logit) * causal[None]
    score_matrix = jnp.einsum('hti,ihm->thm', affinity, softmax_probabilities, precision=running_peak_logit)
    score_matrix = (score_matrix + jnp.einsum('oyq,yiq->oyi', query_matrix, slot_key_state, precision=running_peak_logit)) / running_totals
    raised = jnp.exp(score_matrix - lax.optimization_barrier(jnp.max(score_matrix, axis=-1, keepdims=True)))
    chances = raised / lax.optimization_barrier(jnp.sum(raised, axis=-1, keepdims=True))
    token_segment_part = chances / running_totals
    spread_back = jnp.einsum('thm,ihm->hti', token_segment_part, softmax_probabilities, precision=running_peak_logit) * causal[None]
    attended_output = jnp.einsum('hti,ihd->thd', spread_back, value_matrix, precision=running_peak_logit)
    attended_output = attended_output + jnp.einsum('oki,kis->oks', token_segment_part, slot_value_state, precision=running_peak_logit)
    slot_key_state = slot_key_state + jnp.einsum('lez,leb->ezb', softmax_probabilities, key_matrix, precision=running_peak_logit)
    slot_value_state = slot_value_state + jnp.einsum('lez,leb->ezb', softmax_probabilities, value_matrix, precision=running_peak_logit)
    return ((slot_key_state, slot_value_state, running_totals[-1]), (attended_output, lax.optimization_barrier(jnp.sum(chances, axis=(0, 1)))))

def slot_sequence(segment):
    query_matrix, key_matrix, value_matrix, logits = segment
    length_all = query_matrix.shape[0]
    blocks = length_all // BLOCK

    def to_blocks(array):
        return array.reshape(blocks, BLOCK, array.shape[1], array.shape[2])
    initial = (jnp.zeros((HEADS, SLOTS, DH), jnp.float32), jnp.zeros((HEADS, SLOTS, DH), jnp.float32), jnp.zeros((HEADS, SLOTS), jnp.float32))
    ending, (outputs, masses) = lax.scan(jax.checkpoint(slot_block), initial, (to_blocks(query_matrix), to_blocks(key_matrix), to_blocks(value_matrix), to_blocks(logits)))
    return (outputs.reshape(length_all, HEADS * DH), lax.optimization_barrier(jnp.sum(masses, axis=0)))

def abc_layer(hidden, parameters):
    gains, biases, w_in, w_out, w_up, in_bias, w_down, out_bias = parameters
    row_count = hidden.shape[0]
    head_span = HEADS * DH
    normed = low(normalize(hidden, gains[0], biases[0]))
    projected = low_back(project(normed, w_in))
    sequences = row_count // LEN

    def heads_of(columns, depth):
        return columns.reshape(sequences, LEN, HEADS, depth)
    query_matrix = heads_of(projected[:, :head_span], DH)
    key_matrix = heads_of(projected[:, head_span:2 * head_span], DH)
    value_matrix = heads_of(projected[:, 2 * head_span:3 * head_span], DH)
    logits = heads_of(projected[:, 3 * head_span:], SLOTS)
    outputs, masses = lax.map(slot_sequence, (query_matrix, key_matrix, value_matrix, logits))
    readout = low(outputs.reshape(row_count, head_span))
    middle = hidden + low_back(project(readout, w_out))
    normed_ffn = low(normalize(middle, gains[1], biases[1]))
    inner_act = low_back(project(normed_ffn, w_up)) + in_bias
    active = low(jax.nn.gelu(inner_act, approximate=True))
    result = middle + low_back(project(active, w_down)) + out_bias
    return (result, lax.optimization_barrier(jnp.sum(masses, axis=0)))

def reference(inputs, cotangent, domain_ids, group_of, group_weights, norm_gains, norm_biases, w_in, w_out, w_up, in_bias, w_down, out_bias):
    parameters = tuple((weight_arg.astype(jnp.float32) for weight_arg in (norm_gains, norm_biases, w_in, w_out, w_up, in_bias, w_down, out_bias)))
    seq_weight = group_weights[group_of[domain_ids]]
    scaled = cotangent.astype(jnp.float32) * jnp.repeat(seq_weight, LEN)[:, None]

    def forward(source, probe_input, weights_all):
        layer_zero = tuple((weight_arg[0] for weight_arg in weights_all))
        layer_one = tuple((weight_arg[1] for weight_arg in weights_all))
        middle, mass_zero = abc_layer(source, layer_zero)
        passed = low(low_back(middle + probe_input))
        finished, mass_one = abc_layer(passed, layer_one)
        return (finished, (middle, mass_zero + mass_one))
    source = inputs.astype(jnp.float32)
    finished, pullback, (middle, slot_total) = jax.vjp(forward, source, jnp.zeros_like(source), parameters, has_aux=True)
    grad_source, grad_probe, grad_params = pullback(scaled)
    slot_mass = slot_total / (HEADS * MB * LEN)
    return (jnp.stack([middle, finished]), jnp.stack([grad_source, grad_probe]), grad_params[0], grad_params[1], grad_params[2], grad_params[3], grad_params[4], grad_params[5], grad_params[6], grad_params[7], slot_mass)
```

```python
import functools

import jax
import jax.numpy as jnp
from jax import lax
from jax.experimental import pallas as pl
from jax.experimental.pallas import tpu as pltpu
from jax.sharding import PartitionSpec as P

HEADS = 8
DH = 64
SLOTS = 64
LEN = 1024
D = 512
FF = 2048
PAIRS = HEADS // 2
C = 128
ROWS = 256
STEPS = LEN // ROWS
SUBS = ROWS // C
BACK_STEPS = 2
EPSILON = 1e-05
F32 = jnp.float32
BF16 = jnp.bfloat16
GC = 0.7978845608028654
GA = 0.044715
VMEM_LIMIT = 58 * 1024 * 1024

NN = (((1,), (0,)), ((), ()))
NT = (((1,), (1,)), ((), ()))
TN = (((0,), (0,)), ((), ()))


def mm(a, b, dims=NN):
    return lax.dot_general(a, b, dims, preferred_element_type=F32)


def lane_is_low(shape):
    return lax.broadcasted_iota(jnp.int32, shape, 1) % (2 * DH) < DH


def stack_heads(x):
    low = lane_is_low(x.shape)
    zero = jnp.zeros_like(x)
    return jnp.concatenate([jnp.where(low, x, zero), jnp.where(low, zero, x)], axis=0)


def unstack_heads(y):
    half = y.shape[0] // 2
    return jnp.where(lane_is_low((half, y.shape[1])), y[:half], y[half:])


def causal_pair():
    t = lax.broadcasted_iota(jnp.int32, (C, 2 * C), 0)
    i = lax.broadcasted_iota(jnp.int32, (C, 2 * C), 1) % C
    return t >= i


def block_diag_mask():
    a = lax.broadcasted_iota(jnp.int32, (2 * DH, 2 * DH), 0) // DH
    b = lax.broadcasted_iota(jnp.int32, (2 * DH, 2 * DH), 1) // DH
    return a == b


def half_max(x):
    low = lane_is_low(x.shape)
    m0 = jnp.max(jnp.where(low, x, -jnp.inf), axis=-1, keepdims=True)
    m1 = jnp.max(jnp.where(low, -jnp.inf, x), axis=-1, keepdims=True)
    return jnp.where(low, m0, m1)


def half_sum(x):
    low = lane_is_low(x.shape)
    m0 = jnp.sum(jnp.where(low, x, 0.0), axis=-1, keepdims=True)
    m1 = jnp.sum(jnp.where(low, 0.0, x), axis=-1, keepdims=True)
    return jnp.where(low, m0, m1)


def hat(h):
    center = h - jnp.mean(h, axis=-1, keepdims=True)
    spread = jnp.mean(center * center, axis=-1, keepdims=True)
    r = lax.rsqrt(spread + EPSILON)
    return center * r, r


def norm_back(g_hat, xh, r):
    m1 = jnp.mean(g_hat, axis=-1, keepdims=True)
    m2 = jnp.mean(g_hat * xh, axis=-1, keepdims=True)
    return r * (g_hat - m1 - xh * m2)


def start_weight(is_mine, mine, other, dst, sem):
    @pl.when(is_mine)
    def _():
        pltpu.make_async_copy(mine, dst, sem).start()

    @pl.when(jnp.logical_not(is_mine))
    def _():
        pltpu.make_async_copy(other, dst, sem).start()


def wait_weight(mine, dst, sem):
    pltpu.make_async_copy(mine, dst, sem).wait()


V_GAIN1, V_GAIN2, V_BIAS1, V_BIAS2, V_OUTB, V_INB = 0, 1, 2, 3, 4, 5
VROWS = 16


def in_bias_row(vec_ref):
    return jnp.concatenate([vec_ref[V_INB + i : V_INB + i + 1, :] for i in range(4)], axis=1)


def half_ones():
    return block_diag_mask().astype(BF16)


def two_part(x, y, y_first=False):
    high = x.astype(BF16)
    low = (x - high.astype(F32)).astype(BF16)
    if y_first:
        return mm(y, high) + mm(y, low)
    return mm(high, y) + mm(low, y)


def split(x):
    high = x.astype(BF16)
    return high, (x - high.astype(F32)).astype(BF16)


def first_scores(n1, w_in_v, center, n_first, z_first):
    ok = causal_pair()
    tril = (
        lax.broadcasted_iota(jnp.int32, (C, C), 0) >= lax.broadcasted_iota(jnp.int32, (C, C), 1)
    ).astype(BF16)
    qh, ql = split(mm(n1, w_in_v[:, :D]))
    kh, kl = split(mm(n1, w_in_v[:, D : 2 * D]) - center[0:1, :])
    eh, el = split(jnp.exp(mm(n1, w_in_v[:, 3 * D : 4 * D])))
    z_first[...] = mm(tril, eh) + mm(tril, el)
    for p in range(PAIRS):
        cols = slice(p * 128, (p + 1) * 128)
        ks_h, ks_l = stack_heads(kh[:, cols]), stack_heads(kl[:, cols])
        es_h, es_l = stack_heads(eh[:, cols]), stack_heads(el[:, cols])
        aff = mm(qh[:, cols], ks_h, NT) + mm(qh[:, cols], ks_l, NT) + mm(ql[:, cols], ks_h, NT)
        ah, al = split(jnp.where(ok, aff, 0.0))
        n_first[p] = mm(ah, es_h) + mm(al, es_h) + mm(ah, es_l)


def attend_block(first, n_first, z_first, qkve, att, stk_out, stv_out, readout, kst, vst, zst, center, mass):
    ok = causal_pair()
    diag = block_diag_mask()
    ones = half_ones()
    tril = (
        lax.broadcasted_iota(jnp.int32, (C, C), 0) >= lax.broadcasted_iota(jnp.int32, (C, C), 1)
    ).astype(BF16)
    tiles = [(s, p) for s in range(SUBS) for p in range(PAIRS)]

    def rows(s):
        return slice(s * C, (s + 1) * C)

    def part(j, s, p):
        return qkve[rows(s), j * D + p * 128 : j * D + (p + 1) * 128]

    aff, add_k, add_v = {}, {}, {}
    for s, p in tiles:
        aff[s, p] = jnp.where(ok, mm(part(0, s, p), stack_heads(part(1, s, p)), NT), 0.0).astype(BF16)
    for s, p in tiles:
        e = part(3, s, p)
        add_k[s, p] = mm(part(1, s, p), e, TN)
        add_v[s, p] = mm(e, part(2, s, p), TN)
    z_rows = {}
    z_last = zst[...]
    for s in range(SUBS):
        z = mm(tril, qkve[rows(s), 3 * D : 4 * D]) + z_last
        if s == 0:
            z = jnp.where(first, z_first[...], z)
        z_last = z[C - 1 : C, :]
        z_rows[s] = 1.0 / z
        att[1, rows(s), :] = z_rows[s]
    zst[...] = z_last
    for p in range(PAIRS):
        k_run, v_run = kst[p], vst[p]
        for s in range(SUBS):
            stk_out[s, p] = k_run.astype(BF16)
            stv_out[s, p] = v_run.astype(BF16)
            k_run = k_run + jnp.where(diag, add_k[s, p], 0.0)
            v_run = v_run + jnp.where(diag, add_v[s, p], 0.0)
        kst[p], vst[p] = k_run, v_run
    weights = {}
    for s, p in tiles:
        cols = slice(p * 128, (p + 1) * 128)
        n = mm(aff[s, p], stack_heads(part(3, s, p))) + mm(part(0, s, p), stk_out[s, p])
        if s == 0:
            n = jnp.where(first, n_first[p], n)
        rz = z_rows[s][:, cols]
        score = n * rz
        raised = jnp.exp(score - half_max(score))
        prob = raised / two_part(raised, ones)
        w = (prob * rz).astype(BF16)
        weights[s, p] = w
        att[0, rows(s), cols] = prob
        att[2, rows(s), cols] = score
        mass[:, cols] += jnp.sum(prob, axis=0, keepdims=True)
    spread = {}
    for s, p in tiles:
        spread[s, p] = jnp.where(ok, mm(weights[s, p], stack_heads(part(3, s, p)), NT), 0.0).astype(BF16)
    for s, p in tiles:
        cols = slice(p * 128, (p + 1) * 128)
        o = mm(spread[s, p], stack_heads(part(2, s, p))) + mm(weights[s, p], stv_out[s, p])
        readout[rows(s), cols] = (o + center[1:2, cols]).astype(BF16)


def forward_front(first, h, vec, w_in_v, w_out_v, n1_out, qkve, att, stk_out, stv_out, readout, kst, vst, zst, center, firsts, mass,
                  wait_in, wait_out):
    @pl.when(first)
    def _():
        kst[...] = jnp.zeros_like(kst)
        vst[...] = jnp.zeros_like(vst)
        zst[...] = jnp.zeros_like(zst)
        mass[...] = jnp.zeros_like(mass)

    xh, _ = hat(h)
    n1 = (xh * vec[V_GAIN1 : V_GAIN1 + 1, :] + vec[V_BIAS1 : V_BIAS1 + 1, :]).astype(BF16)
    n1_out[...] = n1
    wait_in()
    qkve[:, :D] = mm(n1, w_in_v[:, :D]).astype(BF16)
    for j in (1, 2):
        part = mm(n1, w_in_v[:, j * D : (j + 1) * D])

        @pl.when(first)
        def _(j=j, part=part):
            center[j - 1 : j, :] = jnp.mean(part, axis=0, keepdims=True)

        qkve[:, j * D : (j + 1) * D] = (part - center[j - 1 : j, :]).astype(BF16)
    qkve[:, 3 * D : 4 * D] = jnp.exp(mm(n1, w_in_v[:, 3 * D : 4 * D])).astype(BF16)
    @pl.when(first)
    def _():
        first_scores(n1[:C], w_in_v, center, *firsts)

    attend_block(first, *firsts, qkve, att, stk_out, stv_out, readout, kst, vst, zst, center, mass)
    wait_out()
    return h + mm(readout[...], w_out_v[...])


def gelu_both(x):
    x2 = x * x
    t = jnp.tanh(GC * x * (1.0 + GA * x2))
    half = 0.5 * (1.0 + t)
    return x * half, half + 0.5 * x * (1.0 - t * t) * (GC * (1.0 + 3.0 * GA * x2))


def fwd0_kernel(ids, x, vec, wi_m, wi_o, wo_m, wo_o, wu_m, wu_o, wd_m, wd_o,
                out, n1_out, qkve, att, stk_out, stv_out, readout, middle_out, n2_out, act_out, dgl_out, mass,
                wi_v, wo_v, wu_v, wd_v, kst, vst, zst, center, n_first, z_first, sems):
    c = pl.program_id(0)
    first = c == 0

    @pl.when(first)
    def _():
        mine = ids[0] == 0
        start_weight(mine, wi_m, wi_o, wi_v, sems.at[0])
        start_weight(mine, wo_m, wo_o, wo_v, sems.at[1])
        start_weight(mine, wu_m, wu_o, wu_v, sems.at[2])
        start_weight(mine, wd_m, wd_o, wd_v, sems.at[3])

    def waiter(ref, v, i):
        def go():
            @pl.when(first)
            def _():
                wait_weight(ref, v, sems.at[i])
        return go

    h = x[...].astype(F32)
    middle = forward_front(first, h, vec, wi_v, wo_v, n1_out, qkve, att, stk_out, stv_out, readout, kst, vst, zst,
                           center, (n_first, z_first), mass, waiter(wi_m, wi_v, 0), waiter(wo_m, wo_v, 1))
    middle_out[...] = middle
    xh, _ = hat(middle)
    n2 = (xh * vec[V_GAIN2 : V_GAIN2 + 1, :] + vec[V_BIAS2 : V_BIAS2 + 1, :]).astype(BF16)
    n2_out[...] = n2
    waiter(wu_m, wu_v, 2)()
    inb = in_bias_row(vec)
    for j in range(4):
        cols = slice(j * D, (j + 1) * D)
        act, dgl = gelu_both(mm(n2, wu_v[:, cols]) + inb[:, cols])
        act_out[:, cols] = act.astype(BF16)
        dgl_out[:, cols] = dgl.astype(BF16)
    waiter(wd_m, wd_v, 3)()
    out[...] = middle + mm(act_out[...], wd_v[...]) + vec[V_OUTB : V_OUTB + 1, :]


def row_block(width, dtype=None):
    return pl.BlockSpec((ROWS, width), lambda c, ids: (c, 0))


def const_block(shape):
    n = len(shape)
    return pl.BlockSpec(shape, lambda c, ids: (0,) * n)


ANY = pl.BlockSpec(memory_space=pl.ANY)


def attention_out_shapes():
    return [
        jax.ShapeDtypeStruct((LEN, D), BF16),
        jax.ShapeDtypeStruct((LEN, 4 * D), BF16),
        jax.ShapeDtypeStruct((3, LEN, D), F32),
        jax.ShapeDtypeStruct((LEN // C, PAIRS, 128, 128), BF16),
        jax.ShapeDtypeStruct((LEN // C, PAIRS, 128, 128), BF16),
    ]


def attention_out_specs():
    return [
        row_block(D),
        row_block(4 * D),
        pl.BlockSpec((3, ROWS, D), lambda c, ids: (0, c, 0)),
        pl.BlockSpec((SUBS, PAIRS, 128, 128), lambda c, ids: (c, 0, 0, 0)),
        pl.BlockSpec((SUBS, PAIRS, 128, 128), lambda c, ids: (c, 0, 0, 0)),
    ]


def attention_scratch():
    return [
        pltpu.VMEM((PAIRS, 128, 128), F32),
        pltpu.VMEM((PAIRS, 128, 128), F32),
        pltpu.VMEM((1, D), F32),
        pltpu.VMEM((2, D), F32),
        pltpu.VMEM((PAIRS, C, 128), F32),
        pltpu.VMEM((C, D), F32),
    ]


def weight_scratch():
    return [
        pltpu.VMEM((D, 4 * D), BF16),
        pltpu.VMEM((D, D), BF16),
        pltpu.VMEM((D, FF), BF16),
        pltpu.VMEM((FF, D), BF16),
    ]


def call(kernel, scalars, grid, operands, in_specs, out_specs, scratch, out_shape, name, flops, num_bytes, deps=(),
         aliases=None):
    first = len(scalars) + len(operands)

    def body(*refs):
        kernel(*refs[:first], *refs[first + len(deps) :])

    return pl.pallas_call(
        body,
        grid_spec=pltpu.PrefetchScalarGridSpec(
            num_scalar_prefetch=len(scalars),
            grid=grid,
            in_specs=list(in_specs) + [ANY] * len(deps),
            out_specs=list(out_specs),
            scratch_shapes=list(scratch),
        ),
        out_shape=list(out_shape),
        input_output_aliases=aliases or {},
        compiler_params=params(),
        cost_estimate=pl.CostEstimate(flops=int(flops), bytes_accessed=int(num_bytes), transcendentals=0),
        name=name,
    )(*scalars, *operands, *deps)


def params(**kw):
    return pltpu.CompilerParams(vmem_limit_bytes=VMEM_LIMIT, **kw)


def run_fwd0(ids, inputs, vec, weights, deps=()):
    flat = [w for pair in weights for w in pair]
    return call(
        fwd0_kernel, (ids,), (STEPS,), [inputs, vec, *flat],
        [pl.BlockSpec((ROWS, D), lambda c, ids: (ids[0] * STEPS + c, 0)), const_block((VROWS, D))] + [ANY] * 8,
        [row_block(D)] + attention_out_specs()
            + [row_block(D), row_block(D), row_block(D), row_block(FF), row_block(FF), const_block((1, D))],
        weight_scratch() + attention_scratch() + [pltpu.SemaphoreType.DMA((4,))],
        [jax.ShapeDtypeStruct((LEN, D), F32)] + attention_out_shapes()
        + [
            jax.ShapeDtypeStruct((LEN, D), BF16),
            jax.ShapeDtypeStruct((LEN, D), F32),
            jax.ShapeDtypeStruct((LEN, D), BF16),
            jax.ShapeDtypeStruct((LEN, FF), BF16),
            jax.ShapeDtypeStruct((LEN, FF), BF16),
            jax.ShapeDtypeStruct((1, D), F32),
        ],
        "forward0", 15000000000.0, 33000000.0, deps)


def ffn_back(go, middle, act, dgl, vec, wo_v, wu_v, wd_v, small):
    go_low = go.astype(BF16)
    inner_cols = []
    for j in range(4):
        cols = slice(j * D, (j + 1) * D)
        d_in = mm(go_low, wd_v[cols, :], NT) * dgl[:, cols].astype(F32)
        small[V_INB + j : V_INB + j + 1, :] += jnp.sum(d_in, axis=0, keepdims=True)
        inner_cols.append(d_in.astype(BF16))
    inner_low = jnp.concatenate(inner_cols, axis=1)
    small[V_OUTB : V_OUTB + 1, :] += jnp.sum(go, axis=0, keepdims=True)
    g2 = mm(inner_low, wu_v[...], NT)
    xh, r = hat(middle)
    small[V_GAIN2 : V_GAIN2 + 1, :] += jnp.sum(g2 * xh, axis=0, keepdims=True)
    small[V_BIAS2 : V_BIAS2 + 1, :] += jnp.sum(g2, axis=0, keepdims=True)
    g_mid = go + norm_back(g2 * vec[V_GAIN2 : V_GAIN2 + 1, :], xh, r)
    mid_low = g_mid.astype(BF16)
    return go_low, g_mid, inner_low, mid_low, mm(mid_low, wo_v[...], NT)


FFN_R = 144


def position(rel, core):
    y, x, far, near = rel & 8, rel & 4, rel & 2, rel & 1
    return jnp.where(core == 1, y | (near * 4) | far | (x // 4), (x * 2) | (y // 2) | far | near)


def cost(flops, num_bytes):
    return pl.CostEstimate(flops=int(flops), bytes_accessed=int(num_bytes), transcendentals=0)


def emit_ffn_grads(ids, n2_all, inner_all, act_all, go_all, rd_all, mid_all, keep, send):
    sec, code = ids[0], ids[1]
    for t, dst in ((1, send), (0, keep)):
        half = jnp.where(sec == t, 0, 1)
        spot = [position(j ^ code, half) for j in range(16)]
        n2h = n2_all[:, pl.ds(pl.multiple_of(half * 256, 256), 256)]
        acc = mm(n2h, inner_all[...], TN)
        for j in range(16):
            for cg in range(4):
                dst[spot[j], cg * 16 : (cg + 1) * 16, :] = acc[j * 16 : (j + 1) * 16, cg * 512 : (cg + 1) * 512].astype(BF16)
        rdh = rd_all[:, pl.ds(pl.multiple_of(half * 256, 256), 256)]
        acc = mm(rdh, mid_all[...], TN)
        for j in range(16):
            dst[spot[j], 64:80, :] = acc[j * 16 : (j + 1) * 16, :].astype(BF16)
        acth = act_all[:, pl.ds(pl.multiple_of(half * 1024, 1024), 1024)]
        acc = mm(acth, go_all[...], TN)
        for j in range(16):
            dst[spot[j], 80:144, :] = acc[j * 64 : (j + 1) * 64, :].astype(BF16)


def fwd1_kernel(ids, wseq, x, cot, vec, wi_m, wi_o, wo_m, wo_o, wu_m, wu_o, wd_m, wd_o,
                out, n1_out, qkve, att, stk_out, stv_out, gmid_out, do_out, mass, small, keep, send,
                wi_v, wo_v, wu_v, wd_v, kst, vst, zst, center, n_first, z_first, rd_all, n2_all, act_all, inner_all, go_all, mid_all, dgl_v, sems):
    c = pl.program_id(0)
    first = c == 0

    @pl.when(first)
    def _():
        mine = ids[0] == 1
        start_weight(mine, wi_m, wi_o, wi_v, sems.at[0])
        start_weight(mine, wo_m, wo_o, wo_v, sems.at[1])
        start_weight(mine, wu_m, wu_o, wu_v, sems.at[2])
        start_weight(mine, wd_m, wd_o, wd_v, sems.at[3])
        small[...] = jnp.zeros_like(small)

    def waiter(ref, v, i):
        def go():
            @pl.when(first)
            def _():
                wait_weight(ref, v, sems.at[i])
        return go

    rows = pl.ds(pl.multiple_of(c * ROWS, ROWS), ROWS)
    h = x[...].astype(BF16).astype(F32)
    readout = rd_all.at[rows, :]
    middle = forward_front(first, h, vec, wi_v, wo_v, n1_out, qkve, att, stk_out, stv_out, readout, kst, vst, zst,
                           center, (n_first, z_first), mass, waiter(wi_m, wi_v, 0), waiter(wo_m, wo_v, 1))
    xh, _ = hat(middle)
    n2 = (xh * vec[V_GAIN2 : V_GAIN2 + 1, :] + vec[V_BIAS2 : V_BIAS2 + 1, :]).astype(BF16)
    n2_all[rows, :] = n2
    waiter(wu_m, wu_v, 2)()
    inb = in_bias_row(vec)
    for j in range(4):
        cols = slice(j * D, (j + 1) * D)
        act, dgl = gelu_both(mm(n2, wu_v[:, cols]) + inb[:, cols])
        act_all[rows, cols] = act.astype(BF16)
        dgl_v[:, cols] = dgl.astype(BF16)
    waiter(wd_m, wd_v, 3)()
    out[...] = middle + mm(act_all[rows, :], wd_v[...]) + vec[V_OUTB : V_OUTB + 1, :]
    go = cot[...].astype(F32) * wseq[0]
    go_low, g_mid, inner_low, mid_low, g_rd = ffn_back(go, middle, act_all, dgl_v, vec, wo_v, wu_v, wd_v, small)
    go_all[rows, :] = go_low
    inner_all[rows, :] = inner_low
    mid_all[rows, :] = mid_low
    gmid_out[...] = g_mid
    do_out[...] = g_rd.astype(BF16)

    @pl.when(c == STEPS - 1)
    def _():
        emit_ffn_grads(ids, n2_all, inner_all, act_all, go_all, rd_all, mid_all, keep, send)


def run_fwd1(ids, wseq, out0, cot, vec, weights, deps=()):
    flat = [w for pair in weights for w in pair]
    return call(
        fwd1_kernel, (ids, wseq), (STEPS,), [out0, cot, vec, *flat],
        [
                pl.BlockSpec((ROWS, D), lambda c, ids, w: (c, 0)),
                pl.BlockSpec((ROWS, D), lambda c, ids, w: (ids[0] * STEPS + c, 0)),
                pl.BlockSpec((VROWS, D), lambda c, ids, w: (0, 0)),
            ] + [ANY] * 8,
        [two(s) for s in [row_block(D)] + attention_out_specs()
                       + [row_block(D), row_block(D), const_block((1, D)), const_block((VROWS, D)),
                          const_block((16, FFN_R, 512)), const_block((16, FFN_R, 512))]],
        weight_scratch() + attention_scratch() + [
                pltpu.VMEM((LEN, D), BF16),
                pltpu.VMEM((LEN, D), BF16),
                pltpu.VMEM((LEN, FF), BF16),
                pltpu.VMEM((LEN, FF), BF16),
                pltpu.VMEM((LEN, D), BF16),
                pltpu.VMEM((LEN, D), BF16),
                pltpu.VMEM((ROWS, FF), BF16),
                pltpu.SemaphoreType.DMA((4,))],
        [jax.ShapeDtypeStruct((LEN, D), F32)] + attention_out_shapes()
        + [
            jax.ShapeDtypeStruct((LEN, D), F32),
            jax.ShapeDtypeStruct((LEN, D), BF16),
            jax.ShapeDtypeStruct((1, D), F32),
            jax.ShapeDtypeStruct((VROWS, D), F32),
            jax.ShapeDtypeStruct((16, FFN_R, 512), BF16),
            jax.ShapeDtypeStruct((16, FFN_R, 512), BF16),
        ],
        "forward1", 25000000000.0, 33000000.0, deps)


def two(spec):
    old = spec.index_map
    return pl.BlockSpec(spec.block_shape, lambda c, ids, w: old(c, ids))


def ffn0_kernel(ids, go, middle, n2, act, dgl, readout, vec, wo_m, wo_o, wu_m, wu_o, wd_m, wd_o,
                gmid_out, do_out, small, keep, send,
                wo_v, wu_v, wd_v, rd_all, n2_all, act_all, inner_all, go_all, mid_all, sems):
    c = pl.program_id(0)
    first = c == 0

    @pl.when(first)
    def _():
        mine = ids[0] == 0
        start_weight(mine, wd_m, wd_o, wd_v, sems.at[2])
        start_weight(mine, wu_m, wu_o, wu_v, sems.at[1])
        start_weight(mine, wo_m, wo_o, wo_v, sems.at[0])
        small[...] = jnp.zeros_like(small)
        wait_weight(wd_m, wd_v, sems.at[2])
        wait_weight(wu_m, wu_v, sems.at[1])
        wait_weight(wo_m, wo_v, sems.at[0])

    rows = pl.ds(pl.multiple_of(c * ROWS, ROWS), ROWS)
    rd_all[rows, :] = readout[...]
    n2_all[rows, :] = n2[...]
    act_all[rows, :] = act[...]
    go_low, g_mid, inner_low, mid_low, g_rd = ffn_back(go[...].astype(F32), middle[...], act, dgl, vec, wo_v, wu_v, wd_v, small)
    go_all[rows, :] = go_low
    inner_all[rows, :] = inner_low
    mid_all[rows, :] = mid_low
    gmid_out[...] = g_mid
    do_out[...] = g_rd.astype(BF16)

    @pl.when(c == STEPS - 1)
    def _():
        emit_ffn_grads(ids, n2_all, inner_all, act_all, go_all, rd_all, mid_all, keep, send)


def run_ffn0(ids, go, middle, n2, act, dgl, readout, vec, weights, deps=()):
    flat = [w for pair in weights for w in pair]
    return call(
        ffn0_kernel, (ids,), (STEPS,), [go, middle, n2, act, dgl, readout, vec, *flat],
        [row_block(D), row_block(D), row_block(D), row_block(FF), row_block(FF), row_block(D),
                      const_block((VROWS, D))] + [ANY] * 6,
        [row_block(D), row_block(D), const_block((VROWS, D)),
                       const_block((16, FFN_R, 512)), const_block((16, FFN_R, 512))],
        weight_scratch()[1:] + [
                pltpu.VMEM((LEN, D), BF16),
                pltpu.VMEM((LEN, D), BF16),
                pltpu.VMEM((LEN, FF), BF16),
                pltpu.VMEM((LEN, FF), BF16),
                pltpu.VMEM((LEN, D), BF16),
                pltpu.VMEM((LEN, D), BF16),
                pltpu.SemaphoreType.DMA((3,))],
        [
            jax.ShapeDtypeStruct((LEN, D), F32),
            jax.ShapeDtypeStruct((LEN, D), BF16),
            jax.ShapeDtypeStruct((VROWS, D), F32),
            jax.ShapeDtypeStruct((16, FFN_R, 512), BF16),
            jax.ShapeDtypeStruct((16, FFN_R, 512), BF16),
        ],
        "backward_ffn0", 12000000000.0, 27000000.0, deps)


def attend_back_block(qkve, att, stk, stv, do, proj_low, gk, gv, gz):
    t_idx = lax.broadcasted_iota(jnp.int32, (C, 2 * C), 0)
    i_idx = lax.broadcasted_iota(jnp.int32, (C, 2 * C), 1) % C
    ok, ok_t = t_idx >= i_idx, t_idx <= i_idx
    diag = block_diag_mask()
    ones = half_ones()
    triu = (
        lax.broadcasted_iota(jnp.int32, (C, C), 0) <= lax.broadcasted_iota(jnp.int32, (C, C), 1)
    ).astype(BF16)
    tiles = [(s, p) for s in reversed(range(SUBS)) for p in range(PAIRS)]

    def rows(s):
        return slice(s * C, (s + 1) * C)

    def part(j, s, p):
        return qkve[rows(s), j * D + p * 128 : j * D + (p + 1) * 128]

    def pair(ref, s, p):
        return ref[rows(s), p * 128 : (p + 1) * 128]

    gov, u_all, w_all, dz_all, add_k, add_v = {}, {}, {}, {}, {}, {}
    for s, p in tiles:
        gov[s, p] = jnp.where(ok, mm(pair(do, s, p), stack_heads(part(2, s, p)), NT), 0.0).astype(BF16)
    for s, p in tiles:
        cols = slice(p * 128, (p + 1) * 128)
        prob, rz, score = (att[j, rows(s), cols] for j in range(3))
        dw = mm(gov[s, p], stack_heads(part(3, s, p))) + mm(pair(do, s, p), stv[s, p], NT)
        t = prob * (dw * rz)
        d_score = t - prob * two_part(t, ones)
        u_all[s, p] = (d_score * rz).astype(BF16)
        w_all[s, p] = (prob * rz).astype(BF16)
        dz_all[s, p] = -(w_all[s, p].astype(F32) * (dw * rz) + u_all[s, p].astype(F32) * score)
    for s, p in tiles:
        add_k[s, p] = mm(u_all[s, p], part(0, s, p), TN)
        add_v[s, p] = mm(w_all[s, p], pair(do, s, p), TN)
    gk_low, gv_low, dz_sum = {}, {}, {}
    for p in range(PAIRS):
        cols = slice(p * 128, (p + 1) * 128)
        k_run, v_run, z_run = gk[p], gv[p], gz[:, cols]
        for s in reversed(range(SUBS)):
            gk_low[s, p], gv_low[s, p] = k_run.astype(BF16), v_run.astype(BF16)
            k_run = k_run + jnp.where(diag, add_k[s, p], 0.0)
            v_run = v_run + jnp.where(diag, add_v[s, p], 0.0)
            dz_sum[s, p] = two_part(dz_all[s, p], triu, True) + z_run
            z_run = dz_sum[s, p][0:1, :]
        gk[p], gv[p], gz[:, cols] = k_run, v_run, z_run
    for s, p in tiles:
        q, k, v, e = (part(j, s, p) for j in range(4))
        g_o = pair(do, s, p)
        w, u = w_all[s, p], u_all[s, p]
        us, ws, qs, gos = stack_heads(u), stack_heads(w), stack_heads(q), stack_heads(g_o)
        d = jnp.where(ok, mm(u, stack_heads(e), NT), 0.0).astype(BF16)
        dq = mm(d, stack_heads(k)) + mm(u, stk[s, p], NT)
        d_t = jnp.where(ok_t, mm(e, us, NT), 0.0).astype(BF16)
        dk = mm(d_t, qs) + mm(e, gk_low[s, p])
        b_t = jnp.where(ok_t, mm(e, ws, NT), 0.0).astype(BF16)
        dv = mm(b_t, gos) + mm(e, gv_low[s, p])
        a_t = jnp.where(ok_t, mm(k, qs, NT), 0.0).astype(BF16)
        g_t = jnp.where(ok_t, mm(v, gos, NT), 0.0).astype(BF16)
        de = mm(a_t, us) + mm(g_t, ws) + dz_sum[s, p] + mm(v, gv_low[s, p], NT) + mm(k, gk_low[s, p], NT)
        proj_low[rows(s), p * 128 : (p + 1) * 128] = dq.astype(BF16)
        proj_low[rows(s), D + p * 128 : D + (p + 1) * 128] = dk.astype(BF16)
        proj_low[rows(s), 2 * D + p * 128 : 2 * D + (p + 1) * 128] = dv.astype(BF16)
        proj_low[rows(s), 3 * D + p * 128 : 3 * D + (p + 1) * 128] = (de * e.astype(F32)).astype(BF16)


WIN_R = 64


def attn_back_kernel(layer, carried, *refs):
    ids, x, qkve, att, stk, stv, do, gmid, vec, wi_m, wi_o = refs[:11]
    gh_out, proj_low, gk_out, gv_out, gz_out, small, wi_v, gk, gv, gz, sems = refs[-11:]
    first = pl.program_id(0) == 0

    @pl.when(first)
    def _():
        start_weight(ids[0] == layer, wi_m, wi_o, wi_v, sems.at[0])
        if carried:
            gk_in, gv_in, gz_in, small_in = refs[11:15]
            gk[...], gv[...], gz[...], small[...] = gk_in[...], gv_in[...], gz_in[...], small_in[...]
        else:
            for ref in (small, gk, gv, gz):
                ref[...] = jnp.zeros_like(ref)

    attend_back_block(qkve, att, stk, stv, do, proj_low, gk, gv, gz)

    @pl.when(first)
    def _():
        wait_weight(wi_m, wi_v, sems.at[0])

    g1 = mm(proj_low[...], wi_v[...], NT)
    h = x[...].astype(BF16).astype(F32)
    xh, r = hat(h)
    small[V_GAIN1 : V_GAIN1 + 1, :] += jnp.sum(g1 * xh, axis=0, keepdims=True)
    small[V_BIAS1 : V_BIAS1 + 1, :] += jnp.sum(g1, axis=0, keepdims=True)
    gh = gmid[...] + norm_back(g1 * vec[V_GAIN1 : V_GAIN1 + 1, :], xh, r)
    gh_out[...] = gh.astype(gh_out.dtype)
    gk_out[...], gv_out[...], gz_out[...] = gk[...], gv[...], gz[...]


def run_attn_back(layer, top, steps, carry, ids, x, qkve, att, stk, stv, do, gmid, vec, weight, deps=()):
    def back(width):
        return pl.BlockSpec((ROWS, width), lambda c, ids: (top - 1 - c, 0))

    if layer == 0:
        x_spec = pl.BlockSpec((ROWS, D), lambda c, ids: (ids[0] * STEPS + top - 1 - c, 0))
    else:
        x_spec = back(D)
    state = pl.BlockSpec((SUBS, PAIRS, 128, 128), lambda c, ids: (top - 1 - c, 0, 0, 0))
    carry_shapes = [(PAIRS, 128, 128), (PAIRS, 128, 128), (1, D), (VROWS, D)]
    in_specs = [x_spec, back(4 * D), pl.BlockSpec((3, ROWS, D), lambda c, ids: (0, top - 1 - c, 0)),
                state, state, back(D), back(D), const_block((VROWS, D)), ANY, ANY]
    operands = [x, qkve, att, stk, stv, do, gmid, vec, *weight]
    aliases = {}
    if carry is not None:
        gh, proj, *small_carry = carry
        in_specs = in_specs + [const_block(shape) for shape in carry_shapes] + [ANY, ANY]
        operands = operands + small_carry + [gh, proj]
        aliases = {len(operands) - 1: 0, len(operands): 1}
    return call(
        functools.partial(attn_back_kernel, layer, carry is not None), (ids,), (steps,), operands,
        in_specs,
        [back(D), back(4 * D)] + [const_block(shape) for shape in carry_shapes],
        [pltpu.VMEM((D, 4 * D), BF16)] + attention_scratch()[:3] + [pltpu.SemaphoreType.DMA((1,))],
        [
            jax.ShapeDtypeStruct((LEN, D), F32 if layer == 0 else BF16),
            jax.ShapeDtypeStruct((LEN, 4 * D), BF16),
        ] + [jax.ShapeDtypeStruct(shape, F32) for shape in carry_shapes],
        f"backward_attention{layer}", 9e9 * steps / STEPS, 17e6 * steps / STEPS, deps, aliases)


def in_grad_kernel(ids, n1, proj, keep, send):
    sec, code = ids[0], ids[1]
    for t, dst in ((1, send), (0, keep)):
        half = jnp.where(sec == t, 0, 1)
        n1h = n1[:, pl.ds(pl.multiple_of(half * 256, 256), 256)]
        acc = mm(n1h, proj[...], TN)
        for j in range(16):
            spot = position(j ^ code, half)
            for cg in range(4):
                dst[spot, cg * 16 : (cg + 1) * 16, :] = acc[j * 16 : (j + 1) * 16, cg * 512 : (cg + 1) * 512].astype(BF16)


def run_in_grad(ids, n1, proj, deps=()):
    shape = (16, WIN_R, 512)
    return call(
        in_grad_kernel, (ids,), (1,), [n1, proj],
        [const_block((LEN, D)), const_block((LEN, 4 * D))],
        [const_block(shape), const_block(shape)],
        [],
        [jax.ShapeDtypeStruct(shape, BF16)] * 2,
        "in_grad", 2200000000.0, 7000000.0, deps)


def compute(ids, wseq, inputs, cot, vec0, vec1, weights, comm=None):
    step = comm.step if comm else lambda token: ()
    start = comm.start if comm else lambda *a: None

    def attn_back(layer, token, x, qkve, att, stk, stv, do, gmid, vec):
        carry, top = None, STEPS
        while top > 0:
            carry = run_attn_back(layer, top, BACK_STEPS, carry, ids, x, qkve, att, stk, stv, do, gmid, vec, weights[0],
                                  deps=step(token))
            token = carry[5]
            top -= BACK_STEPS
        return carry[0], carry[1], carry[5]

    (out0, n1, qkve, att, stk, stv, rd, mid, n2, act, dgl, mass0) = run_fwd0(ids, inputs, vec0, weights, deps=step(None))
    (out1, n1b, qkveb, attb, stkb, stvb, gmid1, do1, mass1, small1a, *f1) = run_fwd1(
        ids, wseq, out0, cot, vec1, weights, deps=step(mass0))
    start("f1", f1)
    start("outputs", out0, out1)
    gh1, proj1, small1b = attn_back(1, mass1, out0, qkveb, attb, stkb, stvb, do1, gmid1, vec1)
    a1 = run_in_grad(ids, n1b, proj1, deps=step(small1b))
    gmid0, do0, small0a, *f0 = run_ffn0(ids, gh1, mid, n2, act, dgl, rd, vec0, weights[1:], deps=step(a1[0]))
    start("mix", a1, f0)
    gh0, proj0, small0b = attn_back(0, small0a, inputs, qkve, att, stk, stv, do0, gmid0, vec0)
    a0 = run_in_grad(ids, n1, proj0)
    step(a0[0])
    start("a0", a0)
    return (out0, out1, gh0, gh1, mass0 + mass1, small0a + small0b, small1a + small1b, f0, a0, f1, a1)


class Transfers:
    def __init__(self):
        self.active, self.results = [], {}

    def start(self, name, *parts):
        if name == "outputs":
            first, second = parts
            self.results[name] = (first, to_core(first, 0), second, to_core(second, 1))
            return
        self.results[name] = []
        if name == "small":
            self.active.append([sum_small(*parts, self.results[name]), False])
            return
        core = {"0": 0, "1": 1}.get(name[-1])
        phase = sum_phase(parts, core, self.results[name])
        self.active.append([phase, False])

    def step(self, token):
        deps = []
        for entry in reversed(self.active):
            phase, begun = entry
            try:
                deps.extend(phase.send(token if begun else None))
            except StopIteration:
                pass
            entry[1] = True
        return deps

    def finish(self, work):
        ready = []
        for _ in range(12):
            made = work(self.results)
            ready = self.step(ready + ([] if made is None else [made]))


def cores_swap(x):
    return lax.ppermute(x, "section", [(0, 1), (1, 0)])


def to_core(x, core):
    return lax.ppermute(x, "section", [(1 - core, core)])


def exchange(x, axis, by):
    return lax.ppermute(x, axis, [(i, i ^ by) for i in range(lax.axis_size(axis))])


def add_low(*terms):
    total = terms[0].astype(F32)
    for term in terms[1:]:
        total = total + term.astype(F32)
    return total.astype(BF16)


def exchange_by_core(x, *by):
    dp, rep = lax.axis_size("dp"), lax.axis_size("rep")
    pairs = [
        ((s * dp + z) * rep + r, (s * dp + (z ^ by[s][1])) * rep + (r ^ by[s][0]))
        for s in range(2) for z in range(dp) for r in range(rep)
    ]
    return lax.ppermute(x, ("section", "dp", "rep"), pairs)


FIRST = ((1, 0), (2, 0))
SECOND = ((2, 0), (0, 1))
THIRD = ((0, 1), (1, 0))


def after(token, *arrays):
    tokens = token if isinstance(token, list) else [] if token is None else [token]
    if not tokens:
        return arrays
    return lax.optimization_barrier((*arrays, *tokens))[: len(arrays)]


def sum_phase(parts, core, result):
    keep = parts[0][0] if len(parts) == 1 else jnp.concatenate([k for k, _ in parts], axis=1)
    send = parts[0][1] if len(parts) == 1 else jnp.concatenate([s for _, s in parts], axis=1)
    got = cores_swap(send)
    token = yield [keep]
    (got,) = after(token, got)
    away, home = add_low(keep[8:], got[8:]), add_low(keep[:8], got[:8])
    got = exchange_by_core(away, *FIRST)
    token = yield [away, home]
    (got,) = after(token, got)
    away, home = add_low(home[4:], got[4:]), add_low(home[:4], got[:4])
    got = exchange_by_core(away, *SECOND)
    token = yield [away, home]
    (got,) = after(token, got)
    home, got = (x.reshape(2, 2, *x.shape[1:]) for x in (home, got))
    away, home = add_low(home[:, 1], got[:, 1]), add_low(home[:, 0], got[:, 0])
    got = exchange_by_core(away, *THIRD)
    token = yield [away, home]
    (got,) = after(token, got)
    away, home = add_low(home[1], got[1]), add_low(home[0], got[0])
    got = exchange(away, "dp", 2)
    token = yield [away, home]
    (got,) = after(token, got)
    s = add_low(home, got)
    bit = 4
    while bit < lax.axis_size("dp"):
        s = add_low(s, exchange(s, "dp", bit))
        bit *= 2
    got = exchange(s, "dp", 2)
    token = yield [s]
    (got,) = after(token, got)
    s = jnp.stack([s, got])
    got = exchange_by_core(s, *THIRD)
    token = yield [s]
    (got,) = after(token, got)
    s = jnp.stack([s, got], axis=1).reshape(4, *s.shape[1:])
    got = exchange_by_core(s, *SECOND)
    token = yield [s]
    (got,) = after(token, got)
    low = jnp.concatenate([s, got], axis=0)
    high = exchange_by_core(low, *FIRST)
    send_on = cores_swap if core is None else lambda x: to_core(x, core)
    far_low = send_on(low)
    token = yield [low]
    (high,) = after(token, high)
    result.extend([low, high, far_low, send_on(high)])
    yield [high]


def sum_small(x, result):
    for axis in ("section", "rep", "dp"):
        bit = 1
        while bit < lax.axis_size(axis):
            got = exchange(x, axis, bit)
            token = yield [x]
            (got,) = after(token, got)
            x = x + got
            bit *= 2
    result.append(x)
    yield [x]


def pick_source(ids, h, own0, recv0, own1, recv1, body):
    layer_one = ids[0] == 1
    own_half = h == ids[0]
    for src, use in (
        (own0, jnp.logical_and(jnp.logical_not(layer_one), own_half)),
        (recv0, jnp.logical_and(jnp.logical_not(layer_one), jnp.logical_not(own_half))),
        (own1, jnp.logical_and(layer_one, own_half)),
        (recv1, jnp.logical_and(layer_one, jnp.logical_not(own_half))),
    ):
        @pl.when(use)
        def _(src=src):
            body(src)


def source_specs(shape, inner):
    rest = (0,) * (len(shape) - 1)

    def spec(layer, own):
        def index(h, i, ids):
            used = jnp.logical_and(ids[0] == layer, (h == ids[0]) == own)
            return (jnp.where(used, inner(i, ids), 0),) + rest

        return pl.BlockSpec(shape, index)

    return [spec(0, True), spec(0, False), spec(1, True), spec(1, False)]


def unpack_kernel(store, offsets, ids, *refs):
    sources, outs, (buf, sems) = refs[:8], refs[8:-2], refs[-2:]
    sec, code = ids[0], ids[1]
    h = pl.program_id(0)

    def fetch(half, slot, start):
        for k, part in enumerate(sources):
            layer, received, upper = k // 4, (k // 2) % 2, k % 2
            def copy(part=part, upper=upper, layer=layer):
                src = part.at[:, pl.ds(offsets[layer], buf.shape[2]), :]
                return pltpu.make_async_copy(src, buf.at[slot, pl.ds(8 * upper, 8)], sems.at[slot, upper])

            if start:
                @pl.when(jnp.logical_and(sec == layer, (half == sec) == (received == 0)))
                def _(copy=copy):
                    copy().start()
            elif k < 2:
                copy().wait()

    @pl.when(h == 0)
    def _():
        fetch(0, 0, True)
        fetch(1, 1, True)

    fetch(h, h, False)
    for j in range(16):
        store(j, buf.at[h, position(j ^ code, h)], outs)


def store_ffn(j, src, outs):
    up, out, down = outs
    for cg in range(4):
        up[j * 16 : (j + 1) * 16, cg * 512 : (cg + 1) * 512] = src[cg * 16 : (cg + 1) * 16, :].astype(F32)
    out[j * 16 : (j + 1) * 16, :] = src[64:80, :].astype(F32)
    down[j * 64 : (j + 1) * 64, :] = src[80:144, :].astype(F32)


def store_in(j, src, outs):
    for cg in range(4):
        outs[0][j * 16 : (j + 1) * 16, cg * 512 : (cg + 1) * 512] = src[cg * 16 : (cg + 1) * 16, :].astype(F32)


def unpack(ids, sources, store, shapes, rows, offsets, name, deps=()):
    return call(
        functools.partial(unpack_kernel, store, offsets), (ids,), (2,), sources,
        [ANY] * 8,
        [pl.BlockSpec((shape[0] // 2, shape[1]), lambda h, ids: (h, 0)) for shape in shapes],
        [pltpu.VMEM((2, 16, rows, 512), BF16), pltpu.SemaphoreType.DMA((2, 2))],
        [jax.ShapeDtypeStruct(shape, F32) for shape in shapes],
        name, 1000000.0, 3 * 4 * 8192 * rows, deps)


def assemble_kernel(ids, own0, recv0, own1, recv1, out):
    def body(src):
        out[...] = src[...].astype(F32)

    pick_source(ids, pl.program_id(0), own0, recv0, own1, recv1, body)


def assemble(ids, sources, name, deps=()):
    return call(
        assemble_kernel, (ids,), (2, 2), sources,
        source_specs((512, D), lambda i, ids: i),
        [pl.BlockSpec((512, D), lambda h, i, ids: (h * 2 + i, 0))],
        [],
        [jax.ShapeDtypeStruct((2 * LEN, D), F32)],
        name, 1000000.0, 8000000.0, deps)[0]


def pack_vectors(norm_gains, norm_biases, in_bias, out_bias):
    rows = [norm_gains[0], norm_biases[0], out_bias, in_bias.reshape(4, D)]
    used = sum(r.shape[0] for r in rows)
    return jnp.concatenate(rows + [jnp.zeros((VROWS - used, D), BF16)], axis=0)


def per_device(inputs, cotangent, domain_ids, group_of, group_weights, norm_gains, norm_biases,
               w_in, w_out, w_up, in_bias, w_down, out_bias):
    sec = lax.axis_index("section")
    code = lax.axis_index("rep") * 4 + lax.axis_index("dp") % 4
    ids = jnp.stack([sec, code]).astype(jnp.int32)
    leading = sec == 0
    mine = [w_in[0], w_out[0], w_up[0], w_down[0]]
    vec_mine = pack_vectors(norm_gains, norm_biases, in_bias, out_bias)
    vec_other = cores_swap(vec_mine)
    weights = [(w, cores_swap(w)) for w in mine]
    vec0 = jnp.where(leading, vec_mine, vec_other).astype(F32)
    vec1 = jnp.where(leading, vec_other, vec_mine).astype(F32)
    own_id = jnp.where(leading, domain_ids[0], domain_ids[1])
    domain_hit = own_id == jnp.arange(group_of.shape[0])
    group = jnp.sum(jnp.where(domain_hit, group_of, 0))
    wseq = jnp.sum(jnp.where(group == jnp.arange(group_weights.shape[0]), group_weights, 0.0)).reshape(1)

    comm = Transfers()
    (out0, out1, gh0, gh1, mass, small0, small1, *_) = compute(ids, wseq, inputs, cotangent, vec0, vec1, weights, comm)
    made = {}
    comm.results["grads"] = (gh0, to_core(gh0, 0), gh1, to_core(gh1, 1))

    def work(got):
        if "outputs" not in made:
            made["outputs"] = assemble(ids, got["outputs"], "layer_outputs")
            return made["outputs"]
        if "grads" not in made:
            made["grads"] = assemble(ids, got["grads"], "input_grads")
            return made["grads"]
        if "ffn" not in made and got["mix"] and got["f1"]:
            shapes = ((D, FF), (D, D), (FF, D))
            made["ffn"] = unpack(ids, got["mix"] + got["f1"], store_ffn, shapes, FFN_R, (WIN_R, 0), "unpack_ffn")
            return made["ffn"][0]
        return None

    comm.start("small", jnp.concatenate([small0[:9], small1[:9], mass, jnp.zeros((5, D), F32)], axis=0))
    comm.finish(work)
    got = comm.results
    layer_outputs, input_grads = made["outputs"], made["grads"]
    g_up, g_wout, g_down = made["ffn"]
    (g_win,) = unpack(ids, got["a0"] + got["mix"], store_in, ((D, 4 * D),), WIN_R, (0, 0), "unpack_in")

    (total,) = got["small"]
    small = jnp.where(leading, total[:9], total[9:18])
    slot_mass = jnp.sum(total[18].reshape(HEADS, SLOTS), axis=0) / (HEADS * 2 * LEN)
    return (
        layer_outputs[None],
        input_grads[None],
        small[0:2][None],
        small[2:4][None],
        g_win[None],
        g_wout[None],
        g_up[None],
        small[V_INB : V_INB + 4].reshape(1, FF),
        g_down[None],
        small[V_OUTB][None],
        slot_mass,
    )


def solution(mesh):
    return jax.shard_map(
        per_device,
        mesh=mesh,
        in_specs=(
            P(("dp", "rep"), None),
            P(("dp", "rep"), None),
            P(("dp", "rep")),
            P(),
            P(),
            P("section", None, None),
            P("section", None, None),
            P("section", None, None),
            P("section", None, None),
            P("section", None, None),
            P("section", None),
            P("section", None, None),
            P("section", None),
        ),
        out_specs=(
            P("section", ("dp", "rep"), None),
            P("section", ("dp", "rep"), None),
            P("section", None, None),
            P("section", None, None),
            P("section", None, None),
            P("section", None, None),
            P("section", None, None),
            P("section", None),
            P("section", None, None),
            P("section", None),
            P(),
        ),
        check_vma=False,
    )
```

```python
import functools

import jax
import jax.numpy as jnp
from jax import lax
from jax.experimental import pallas as pl
from jax.experimental.pallas import tpu as pltpu
from jax.sharding import PartitionSpec as P

HEADS = 8
DH = 64
SLOTS = 64
LEN = 1024
D = 512
FF = 2048
PAIRS = HEADS // 2
C = 128
ROWS = 256
STEPS = LEN // ROWS
SUBS = ROWS // C
BACK_STEPS = 4
EPSILON = 1e-05
F32 = jnp.float32
BF16 = jnp.bfloat16
GC = 0.7978845608028654
GA = 0.044715
VMEM_LIMIT = 58 * 1024 * 1024

NN = (((1,), (0,)), ((), ()))
NT = (((1,), (1,)), ((), ()))
TN = (((0,), (0,)), ((), ()))


def mm(a, b, dims=NN):
    return lax.dot_general(a, b, dims, preferred_element_type=F32)


def lane_is_low(shape):
    return lax.broadcasted_iota(jnp.int32, shape, 1) % (2 * DH) < DH


def stack_heads(x):
    low = lane_is_low(x.shape)
    zero = jnp.zeros_like(x)
    return jnp.concatenate([jnp.where(low, x, zero), jnp.where(low, zero, x)], axis=0)


def unstack_heads(y):
    half = y.shape[0] // 2
    return jnp.where(lane_is_low((half, y.shape[1])), y[:half], y[half:])


def causal_pair():
    t = lax.broadcasted_iota(jnp.int32, (C, 2 * C), 0)
    i = lax.broadcasted_iota(jnp.int32, (C, 2 * C), 1) % C
    return t >= i


def block_diag_mask():
    a = lax.broadcasted_iota(jnp.int32, (2 * DH, 2 * DH), 0) // DH
    b = lax.broadcasted_iota(jnp.int32, (2 * DH, 2 * DH), 1) // DH
    return a == b


def half_max(x):
    low = lane_is_low(x.shape)
    m0 = jnp.max(jnp.where(low, x, -jnp.inf), axis=-1, keepdims=True)
    m1 = jnp.max(jnp.where(low, -jnp.inf, x), axis=-1, keepdims=True)
    return jnp.where(low, m0, m1)


def half_sum(x):
    low = lane_is_low(x.shape)
    m0 = jnp.sum(jnp.where(low, x, 0.0), axis=-1, keepdims=True)
    m1 = jnp.sum(jnp.where(low, 0.0, x), axis=-1, keepdims=True)
    return jnp.where(low, m0, m1)


def hat(h):
    center = h - jnp.mean(h, axis=-1, keepdims=True)
    spread = jnp.mean(center * center, axis=-1, keepdims=True)
    r = lax.rsqrt(spread + EPSILON)
    return center * r, r


def norm_back(g_hat, xh, r):
    m1 = jnp.mean(g_hat, axis=-1, keepdims=True)
    m2 = jnp.mean(g_hat * xh, axis=-1, keepdims=True)
    return r * (g_hat - m1 - xh * m2)


def start_weight(is_mine, mine, other, dst, sem):
    @pl.when(is_mine)
    def _():
        pltpu.make_async_copy(mine, dst, sem).start()

    @pl.when(jnp.logical_not(is_mine))
    def _():
        pltpu.make_async_copy(other, dst, sem).start()


def wait_weight(mine, dst, sem):
    pltpu.make_async_copy(mine, dst, sem).wait()


V_GAIN1, V_GAIN2, V_BIAS1, V_BIAS2, V_OUTB, V_INB = 0, 1, 2, 3, 4, 5
VROWS = 16


def in_bias_row(vec_ref):
    return jnp.concatenate([vec_ref[V_INB + i : V_INB + i + 1, :] for i in range(4)], axis=1)


def half_ones():
    return block_diag_mask().astype(BF16)


def two_part(x, y, y_first=False):
    high = x.astype(BF16)
    low = (x - high.astype(F32)).astype(BF16)
    if y_first:
        return mm(y, high) + mm(y, low)
    return mm(high, y) + mm(low, y)


def split(x):
    high = x.astype(BF16)
    return high, (x - high.astype(F32)).astype(BF16)


def first_scores(n1, w_in_v, center, n_first, z_first):
    ok = causal_pair()
    tril = (
        lax.broadcasted_iota(jnp.int32, (C, C), 0) >= lax.broadcasted_iota(jnp.int32, (C, C), 1)
    ).astype(BF16)
    qh, ql = split(mm(n1, w_in_v[:, :D]))
    kh, kl = split(mm(n1, w_in_v[:, D : 2 * D]) - center[0:1, :])
    eh, el = split(jnp.exp(mm(n1, w_in_v[:, 3 * D : 4 * D])))
    z_first[...] = mm(tril, eh) + mm(tril, el)
    for p in range(PAIRS):
        cols = slice(p * 128, (p + 1) * 128)
        ks_h, ks_l = stack_heads(kh[:, cols]), stack_heads(kl[:, cols])
        es_h, es_l = stack_heads(eh[:, cols]), stack_heads(el[:, cols])
        aff = mm(qh[:, cols], ks_h, NT) + mm(qh[:, cols], ks_l, NT) + mm(ql[:, cols], ks_h, NT)
        ah, al = split(jnp.where(ok, aff, 0.0))
        n_first[p] = mm(ah, es_h) + mm(al, es_h) + mm(ah, es_l)


def attend_block(first, n_first, z_first, qkve, att, stk_out, stv_out, readout, kst, vst, zst, center, mass):
    ok = causal_pair()
    diag = block_diag_mask()
    ones = half_ones()
    tril = (
        lax.broadcasted_iota(jnp.int32, (C, C), 0) >= lax.broadcasted_iota(jnp.int32, (C, C), 1)
    ).astype(BF16)
    tiles = [(s, p) for s in range(SUBS) for p in range(PAIRS)]

    def rows(s):
        return slice(s * C, (s + 1) * C)

    def part(j, s, p):
        return qkve[rows(s), j * D + p * 128 : j * D + (p + 1) * 128]

    aff, add_k, add_v = {}, {}, {}
    for s, p in tiles:
        aff[s, p] = jnp.where(ok, mm(part(0, s, p), stack_heads(part(1, s, p)), NT), 0.0).astype(BF16)
    for s, p in tiles:
        e = part(3, s, p)
        add_k[s, p] = mm(part(1, s, p), e, TN)
        add_v[s, p] = mm(e, part(2, s, p), TN)
    z_rows = {}
    z_last = zst[...]
    for s in range(SUBS):
        z = mm(tril, qkve[rows(s), 3 * D : 4 * D]) + z_last
        if s == 0:
            z = jnp.where(first, z_first[...], z)
        z_last = z[C - 1 : C, :]
        z_rows[s] = 1.0 / z
        att[1, rows(s), :] = z_rows[s]
    zst[...] = z_last
    for p in range(PAIRS):
        k_run, v_run = kst[p], vst[p]
        for s in range(SUBS):
            stk_out[s, p] = k_run.astype(BF16)
            stv_out[s, p] = v_run.astype(BF16)
            k_run = k_run + jnp.where(diag, add_k[s, p], 0.0)
            v_run = v_run + jnp.where(diag, add_v[s, p], 0.0)
        kst[p], vst[p] = k_run, v_run
    weights = {}
    for s, p in tiles:
        cols = slice(p * 128, (p + 1) * 128)
        n = mm(aff[s, p], stack_heads(part(3, s, p))) + mm(part(0, s, p), stk_out[s, p])
        if s == 0:
            n = jnp.where(first, n_first[p], n)
        rz = z_rows[s][:, cols]
        score = n * rz
        raised = jnp.exp(score - half_max(score))
        prob = raised / two_part(raised, ones)
        w = (prob * rz).astype(BF16)
        weights[s, p] = w
        att[0, rows(s), cols] = prob
        att[2, rows(s), cols] = score
        mass[:, cols] += jnp.sum(prob, axis=0, keepdims=True)
    spread = {}
    for s, p in tiles:
        spread[s, p] = jnp.where(ok, mm(weights[s, p], stack_heads(part(3, s, p)), NT), 0.0).astype(BF16)
    for s, p in tiles:
        cols = slice(p * 128, (p + 1) * 128)
        o = mm(spread[s, p], stack_heads(part(2, s, p))) + mm(weights[s, p], stv_out[s, p])
        readout[rows(s), cols] = (o + center[1:2, cols]).astype(BF16)


def forward_front(first, h, vec, w_in_v, w_out_v, n1_out, qkve, att, stk_out, stv_out, readout, kst, vst, zst, center, firsts, mass,
                  wait_in, wait_out):
    @pl.when(first)
    def _():
        kst[...] = jnp.zeros_like(kst)
        vst[...] = jnp.zeros_like(vst)
        zst[...] = jnp.zeros_like(zst)
        mass[...] = jnp.zeros_like(mass)

    xh, _ = hat(h)
    n1 = (xh * vec[V_GAIN1 : V_GAIN1 + 1, :] + vec[V_BIAS1 : V_BIAS1 + 1, :]).astype(BF16)
    n1_out[...] = n1
    wait_in()
    qkve[:, :D] = mm(n1, w_in_v[:, :D]).astype(BF16)
    for j in (1, 2):
        part = mm(n1, w_in_v[:, j * D : (j + 1) * D])

        @pl.when(first)
        def _(j=j, part=part):
            center[j - 1 : j, :] = jnp.mean(part, axis=0, keepdims=True)

        qkve[:, j * D : (j + 1) * D] = (part - center[j - 1 : j, :]).astype(BF16)
    qkve[:, 3 * D : 4 * D] = jnp.exp(mm(n1, w_in_v[:, 3 * D : 4 * D])).astype(BF16)
    @pl.when(first)
    def _():
        first_scores(n1[:C], w_in_v, center, *firsts)

    attend_block(first, *firsts, qkve, att, stk_out, stv_out, readout, kst, vst, zst, center, mass)
    wait_out()
    return h + mm(readout[...], w_out_v[...])


def gelu_both(x):
    x2 = x * x
    t = jnp.tanh(GC * x * (1.0 + GA * x2))
    half = 0.5 * (1.0 + t)
    return x * half, half + 0.5 * x * (1.0 - t * t) * (GC * (1.0 + 3.0 * GA * x2))


def fwd0_kernel(ids, x, vec, wi_m, wi_o, wo_m, wo_o, wu_m, wu_o, wd_m, wd_o,
                out, n1_out, qkve, att, stk_out, stv_out, readout, middle_out, n2_out, act_out, dgl_out, mass,
                wi_v, wo_v, wu_v, wd_v, kst, vst, zst, center, n_first, z_first, sems):
    c = pl.program_id(0)
    first = c == 0

    @pl.when(first)
    def _():
        mine = ids[0] == 0
        start_weight(mine, wi_m, wi_o, wi_v, sems.at[0])
        start_weight(mine, wo_m, wo_o, wo_v, sems.at[1])
        start_weight(mine, wu_m, wu_o, wu_v, sems.at[2])
        start_weight(mine, wd_m, wd_o, wd_v, sems.at[3])

    def waiter(ref, v, i):
        def go():
            @pl.when(first)
            def _():
                wait_weight(ref, v, sems.at[i])
        return go

    h = x[...].astype(F32)
    middle = forward_front(first, h, vec, wi_v, wo_v, n1_out, qkve, att, stk_out, stv_out, readout, kst, vst, zst,
                           center, (n_first, z_first), mass, waiter(wi_m, wi_v, 0), waiter(wo_m, wo_v, 1))
    middle_out[...] = middle
    xh, _ = hat(middle)
    n2 = (xh * vec[V_GAIN2 : V_GAIN2 + 1, :] + vec[V_BIAS2 : V_BIAS2 + 1, :]).astype(BF16)
    n2_out[...] = n2
    waiter(wu_m, wu_v, 2)()
    inb = in_bias_row(vec)
    for j in range(4):
        cols = slice(j * D, (j + 1) * D)
        act, dgl = gelu_both(mm(n2, wu_v[:, cols]) + inb[:, cols])
        act_out[:, cols] = act.astype(BF16)
        dgl_out[:, cols] = dgl.astype(BF16)
    waiter(wd_m, wd_v, 3)()
    out[...] = middle + mm(act_out[...], wd_v[...]) + vec[V_OUTB : V_OUTB + 1, :]


def row_block(width, dtype=None):
    return pl.BlockSpec((ROWS, width), lambda c, ids: (c, 0))


def const_block(shape):
    n = len(shape)
    return pl.BlockSpec(shape, lambda c, ids: (0,) * n)


ANY = pl.BlockSpec(memory_space=pl.ANY)


def attention_out_shapes():
    return [
        jax.ShapeDtypeStruct((LEN, D), BF16),
        jax.ShapeDtypeStruct((LEN, 4 * D), BF16),
        jax.ShapeDtypeStruct((3, LEN, D), F32),
        jax.ShapeDtypeStruct((LEN // C, PAIRS, 128, 128), BF16),
        jax.ShapeDtypeStruct((LEN // C, PAIRS, 128, 128), BF16),
    ]


def attention_out_specs():
    return [
        row_block(D),
        row_block(4 * D),
        pl.BlockSpec((3, ROWS, D), lambda c, ids: (0, c, 0)),
        pl.BlockSpec((SUBS, PAIRS, 128, 128), lambda c, ids: (c, 0, 0, 0)),
        pl.BlockSpec((SUBS, PAIRS, 128, 128), lambda c, ids: (c, 0, 0, 0)),
    ]


def attention_scratch():
    return [
        pltpu.VMEM((PAIRS, 128, 128), F32),
        pltpu.VMEM((PAIRS, 128, 128), F32),
        pltpu.VMEM((1, D), F32),
        pltpu.VMEM((2, D), F32),
        pltpu.VMEM((PAIRS, C, 128), F32),
        pltpu.VMEM((C, D), F32),
    ]


def weight_scratch():
    return [
        pltpu.VMEM((D, 4 * D), BF16),
        pltpu.VMEM((D, D), BF16),
        pltpu.VMEM((D, FF), BF16),
        pltpu.VMEM((FF, D), BF16),
    ]


def call(kernel, scalars, grid, operands, in_specs, out_specs, scratch, out_shape, name, flops, num_bytes, deps=(),
         aliases=None):
    first = len(scalars) + len(operands)

    def body(*refs):
        kernel(*refs[:first], *refs[first + len(deps) :])

    return pl.pallas_call(
        body,
        grid_spec=pltpu.PrefetchScalarGridSpec(
            num_scalar_prefetch=len(scalars),
            grid=grid,
            in_specs=list(in_specs) + [ANY] * len(deps),
            out_specs=list(out_specs),
            scratch_shapes=list(scratch),
        ),
        out_shape=list(out_shape),
        input_output_aliases=aliases or {},
        compiler_params=params(),
        cost_estimate=pl.CostEstimate(flops=int(flops), bytes_accessed=int(num_bytes), transcendentals=0),
        name=name,
    )(*scalars, *operands, *deps)


def params(**kw):
    return pltpu.CompilerParams(vmem_limit_bytes=VMEM_LIMIT, **kw)


def run_fwd0(ids, inputs, vec, weights, deps=()):
    flat = [w for pair in weights for w in pair]
    return call(
        fwd0_kernel, (ids,), (STEPS,), [inputs, vec, *flat],
        [pl.BlockSpec((ROWS, D), lambda c, ids: (ids[0] * STEPS + c, 0)), const_block((VROWS, D))] + [ANY] * 8,
        [row_block(D)] + attention_out_specs()
            + [row_block(D), row_block(D), row_block(D), row_block(FF), row_block(FF), const_block((1, D))],
        weight_scratch() + attention_scratch() + [pltpu.SemaphoreType.DMA((4,))],
        [jax.ShapeDtypeStruct((LEN, D), F32)] + attention_out_shapes()
        + [
            jax.ShapeDtypeStruct((LEN, D), BF16),
            jax.ShapeDtypeStruct((LEN, D), F32),
            jax.ShapeDtypeStruct((LEN, D), BF16),
            jax.ShapeDtypeStruct((LEN, FF), BF16),
            jax.ShapeDtypeStruct((LEN, FF), BF16),
            jax.ShapeDtypeStruct((1, D), F32),
        ],
        "forward0", 15000000000.0, 33000000.0, deps)


def ffn_back(go, middle, act, dgl, vec, wo_v, wu_v, wd_v, small):
    go_low = go.astype(BF16)
    inner_cols = []
    for j in range(4):
        cols = slice(j * D, (j + 1) * D)
        d_in = mm(go_low, wd_v[cols, :], NT) * dgl[:, cols].astype(F32)
        small[V_INB + j : V_INB + j + 1, :] += jnp.sum(d_in, axis=0, keepdims=True)
        inner_cols.append(d_in.astype(BF16))
    inner_low = jnp.concatenate(inner_cols, axis=1)
    small[V_OUTB : V_OUTB + 1, :] += jnp.sum(go, axis=0, keepdims=True)
    g2 = mm(inner_low, wu_v[...], NT)
    xh, r = hat(middle)
    small[V_GAIN2 : V_GAIN2 + 1, :] += jnp.sum(g2 * xh, axis=0, keepdims=True)
    small[V_BIAS2 : V_BIAS2 + 1, :] += jnp.sum(g2, axis=0, keepdims=True)
    g_mid = go + norm_back(g2 * vec[V_GAIN2 : V_GAIN2 + 1, :], xh, r)
    mid_low = g_mid.astype(BF16)
    return go_low, g_mid, inner_low, mid_low, mm(mid_low, wo_v[...], NT)


FFN_R = 144


def position(rel, core):
    y, x, far, near = rel & 8, rel & 4, rel & 2, rel & 1
    return jnp.where(core == 1, y | (near * 4) | far | (x // 4), (x * 2) | (y // 2) | far | near)


def cost(flops, num_bytes):
    return pl.CostEstimate(flops=int(flops), bytes_accessed=int(num_bytes), transcendentals=0)


def emit_ffn_grads(ids, n2_all, inner_all, act_all, go_all, rd_all, mid_all, keep, send):
    sec, code = ids[0], ids[1]
    for t, dst in ((1, send), (0, keep)):
        half = jnp.where(sec == t, 0, 1)
        spot = [position(j ^ code, half) for j in range(16)]
        n2h = n2_all[:, pl.ds(pl.multiple_of(half * 256, 256), 256)]
        acc = mm(n2h, inner_all[...], TN)
        for j in range(16):
            for cg in range(4):
                dst[spot[j], cg * 16 : (cg + 1) * 16, :] = acc[j * 16 : (j + 1) * 16, cg * 512 : (cg + 1) * 512].astype(BF16)
        rdh = rd_all[:, pl.ds(pl.multiple_of(half * 256, 256), 256)]
        acc = mm(rdh, mid_all[...], TN)
        for j in range(16):
            dst[spot[j], 64:80, :] = acc[j * 16 : (j + 1) * 16, :].astype(BF16)
        acth = act_all[:, pl.ds(pl.multiple_of(half * 1024, 1024), 1024)]
        acc = mm(acth, go_all[...], TN)
        for j in range(16):
            dst[spot[j], 80:144, :] = acc[j * 64 : (j + 1) * 64, :].astype(BF16)


def fwd1_kernel(ids, wseq, x, cot, vec, wi_m, wi_o, wo_m, wo_o, wu_m, wu_o, wd_m, wd_o,
                out, n1_out, qkve, att, stk_out, stv_out, gmid_out, do_out, mass, small, keep, send,
                wi_v, wo_v, wu_v, wd_v, kst, vst, zst, center, n_first, z_first, rd_all, n2_all, act_all, inner_all, go_all, mid_all, dgl_v, sems):
    c = pl.program_id(0)
    first = c == 0

    @pl.when(first)
    def _():
        mine = ids[0] == 1
        start_weight(mine, wi_m, wi_o, wi_v, sems.at[0])
        start_weight(mine, wo_m, wo_o, wo_v, sems.at[1])
        start_weight(mine, wu_m, wu_o, wu_v, sems.at[2])
        start_weight(mine, wd_m, wd_o, wd_v, sems.at[3])
        small[...] = jnp.zeros_like(small)

    def waiter(ref, v, i):
        def go():
            @pl.when(first)
            def _():
                wait_weight(ref, v, sems.at[i])
        return go

    rows = pl.ds(pl.multiple_of(c * ROWS, ROWS), ROWS)
    h = x[...].astype(BF16).astype(F32)
    readout = rd_all.at[rows, :]
    middle = forward_front(first, h, vec, wi_v, wo_v, n1_out, qkve, att, stk_out, stv_out, readout, kst, vst, zst,
                           center, (n_first, z_first), mass, waiter(wi_m, wi_v, 0), waiter(wo_m, wo_v, 1))
    xh, _ = hat(middle)
    n2 = (xh * vec[V_GAIN2 : V_GAIN2 + 1, :] + vec[V_BIAS2 : V_BIAS2 + 1, :]).astype(BF16)
    n2_all[rows, :] = n2
    waiter(wu_m, wu_v, 2)()
    inb = in_bias_row(vec)
    for j in range(4):
        cols = slice(j * D, (j + 1) * D)
        act, dgl = gelu_both(mm(n2, wu_v[:, cols]) + inb[:, cols])
        act_all[rows, cols] = act.astype(BF16)
        dgl_v[:, cols] = dgl.astype(BF16)
    waiter(wd_m, wd_v, 3)()
    out[...] = middle + mm(act_all[rows, :], wd_v[...]) + vec[V_OUTB : V_OUTB + 1, :]
    go = cot[...].astype(F32) * wseq[0]
    go_low, g_mid, inner_low, mid_low, g_rd = ffn_back(go, middle, act_all, dgl_v, vec, wo_v, wu_v, wd_v, small)
    go_all[rows, :] = go_low
    inner_all[rows, :] = inner_low
    mid_all[rows, :] = mid_low
    gmid_out[...] = g_mid
    do_out[...] = g_rd.astype(BF16)

    @pl.when(c == STEPS - 1)
    def _():
        emit_ffn_grads(ids, n2_all, inner_all, act_all, go_all, rd_all, mid_all, keep, send)


def run_fwd1(ids, wseq, out0, cot, vec, weights, deps=()):
    flat = [w for pair in weights for w in pair]
    return call(
        fwd1_kernel, (ids, wseq), (STEPS,), [out0, cot, vec, *flat],
        [
                pl.BlockSpec((ROWS, D), lambda c, ids, w: (c, 0)),
                pl.BlockSpec((ROWS, D), lambda c, ids, w: (ids[0] * STEPS + c, 0)),
                pl.BlockSpec((VROWS, D), lambda c, ids, w: (0, 0)),
            ] + [ANY] * 8,
        [two(s) for s in [row_block(D)] + attention_out_specs()
                       + [row_block(D), row_block(D), const_block((1, D)), const_block((VROWS, D)),
                          const_block((16, FFN_R, 512)), const_block((16, FFN_R, 512))]],
        weight_scratch() + attention_scratch() + [
                pltpu.VMEM((LEN, D), BF16),
                pltpu.VMEM((LEN, D), BF16),
                pltpu.VMEM((LEN, FF), BF16),
                pltpu.VMEM((LEN, FF), BF16),
                pltpu.VMEM((LEN, D), BF16),
                pltpu.VMEM((LEN, D), BF16),
                pltpu.VMEM((ROWS, FF), BF16),
                pltpu.SemaphoreType.DMA((4,))],
        [jax.ShapeDtypeStruct((LEN, D), F32)] + attention_out_shapes()
        + [
            jax.ShapeDtypeStruct((LEN, D), F32),
            jax.ShapeDtypeStruct((LEN, D), BF16),
            jax.ShapeDtypeStruct((1, D), F32),
            jax.ShapeDtypeStruct((VROWS, D), F32),
            jax.ShapeDtypeStruct((16, FFN_R, 512), BF16),
            jax.ShapeDtypeStruct((16, FFN_R, 512), BF16),
        ],
        "forward1", 25000000000.0, 33000000.0, deps)


def two(spec):
    old = spec.index_map
    return pl.BlockSpec(spec.block_shape, lambda c, ids, w: old(c, ids))


def ffn0_kernel(ids, go, middle, n2, act, dgl, readout, vec, wo_m, wo_o, wu_m, wu_o, wd_m, wd_o,
                gmid_out, do_out, small, keep, send,
                wo_v, wu_v, wd_v, rd_all, n2_all, act_all, inner_all, go_all, mid_all, sems):
    c = pl.program_id(0)
    first = c == 0

    @pl.when(first)
    def _():
        mine = ids[0] == 0
        start_weight(mine, wd_m, wd_o, wd_v, sems.at[2])
        start_weight(mine, wu_m, wu_o, wu_v, sems.at[1])
        start_weight(mine, wo_m, wo_o, wo_v, sems.at[0])
        small[...] = jnp.zeros_like(small)
        wait_weight(wd_m, wd_v, sems.at[2])
        wait_weight(wu_m, wu_v, sems.at[1])
        wait_weight(wo_m, wo_v, sems.at[0])

    rows = pl.ds(pl.multiple_of(c * ROWS, ROWS), ROWS)
    rd_all[rows, :] = readout[...]
    n2_all[rows, :] = n2[...]
    act_all[rows, :] = act[...]
    go_low, g_mid, inner_low, mid_low, g_rd = ffn_back(go[...].astype(F32), middle[...], act, dgl, vec, wo_v, wu_v, wd_v, small)
    go_all[rows, :] = go_low
    inner_all[rows, :] = inner_low
    mid_all[rows, :] = mid_low
    gmid_out[...] = g_mid
    do_out[...] = g_rd.astype(BF16)

    @pl.when(c == STEPS - 1)
    def _():
        emit_ffn_grads(ids, n2_all, inner_all, act_all, go_all, rd_all, mid_all, keep, send)


def run_ffn0(ids, go, middle, n2, act, dgl, readout, vec, weights, deps=()):
    flat = [w for pair in weights for w in pair]
    return call(
        ffn0_kernel, (ids,), (STEPS,), [go, middle, n2, act, dgl, readout, vec, *flat],
        [row_block(D), row_block(D), row_block(D), row_block(FF), row_block(FF), row_block(D),
                      const_block((VROWS, D))] + [ANY] * 6,
        [row_block(D), row_block(D), const_block((VROWS, D)),
                       const_block((16, FFN_R, 512)), const_block((16, FFN_R, 512))],
        weight_scratch()[1:] + [
                pltpu.VMEM((LEN, D), BF16),
                pltpu.VMEM((LEN, D), BF16),
                pltpu.VMEM((LEN, FF), BF16),
                pltpu.VMEM((LEN, FF), BF16),
                pltpu.VMEM((LEN, D), BF16),
                pltpu.VMEM((LEN, D), BF16),
                pltpu.SemaphoreType.DMA((3,))],
        [
            jax.ShapeDtypeStruct((LEN, D), F32),
            jax.ShapeDtypeStruct((LEN, D), BF16),
            jax.ShapeDtypeStruct((VROWS, D), F32),
            jax.ShapeDtypeStruct((16, FFN_R, 512), BF16),
            jax.ShapeDtypeStruct((16, FFN_R, 512), BF16),
        ],
        "backward_ffn0", 12000000000.0, 27000000.0, deps)


def attend_back_block(qkve, att, stk, stv, do, proj_low, gk, gv, gz):
    t_idx = lax.broadcasted_iota(jnp.int32, (C, 2 * C), 0)
    i_idx = lax.broadcasted_iota(jnp.int32, (C, 2 * C), 1) % C
    ok, ok_t = t_idx >= i_idx, t_idx <= i_idx
    diag = block_diag_mask()
    ones = half_ones()
    triu = (
        lax.broadcasted_iota(jnp.int32, (C, C), 0) <= lax.broadcasted_iota(jnp.int32, (C, C), 1)
    ).astype(BF16)
    tiles = [(s, p) for s in reversed(range(SUBS)) for p in range(PAIRS)]

    def rows(s):
        return slice(s * C, (s + 1) * C)

    def part(j, s, p):
        return qkve[rows(s), j * D + p * 128 : j * D + (p + 1) * 128]

    def pair(ref, s, p):
        return ref[rows(s), p * 128 : (p + 1) * 128]

    gov, u_all, w_all, dz_all, add_k, add_v = {}, {}, {}, {}, {}, {}
    for s, p in tiles:
        gov[s, p] = jnp.where(ok, mm(pair(do, s, p), stack_heads(part(2, s, p)), NT), 0.0).astype(BF16)
    for s, p in tiles:
        cols = slice(p * 128, (p + 1) * 128)
        prob, rz, score = (att[j, rows(s), cols] for j in range(3))
        dw = mm(gov[s, p], stack_heads(part(3, s, p))) + mm(pair(do, s, p), stv[s, p], NT)
        t = prob * (dw * rz)
        d_score = t - prob * two_part(t, ones)
        u_all[s, p] = (d_score * rz).astype(BF16)
        w_all[s, p] = (prob * rz).astype(BF16)
        dz_all[s, p] = -(w_all[s, p].astype(F32) * (dw * rz) + u_all[s, p].astype(F32) * score)
    for s, p in tiles:
        add_k[s, p] = mm(u_all[s, p], part(0, s, p), TN)
        add_v[s, p] = mm(w_all[s, p], pair(do, s, p), TN)
    gk_low, gv_low, dz_sum = {}, {}, {}
    for p in range(PAIRS):
        cols = slice(p * 128, (p + 1) * 128)
        k_run, v_run, z_run = gk[p], gv[p], gz[:, cols]
        for s in reversed(range(SUBS)):
            gk_low[s, p], gv_low[s, p] = k_run.astype(BF16), v_run.astype(BF16)
            k_run = k_run + jnp.where(diag, add_k[s, p], 0.0)
            v_run = v_run + jnp.where(diag, add_v[s, p], 0.0)
            dz_sum[s, p] = two_part(dz_all[s, p], triu, True) + z_run
            z_run = dz_sum[s, p][0:1, :]
        gk[p], gv[p], gz[:, cols] = k_run, v_run, z_run
    for s, p in tiles:
        q, k, v, e = (part(j, s, p) for j in range(4))
        g_o = pair(do, s, p)
        w, u = w_all[s, p], u_all[s, p]
        us, ws, qs, gos = stack_heads(u), stack_heads(w), stack_heads(q), stack_heads(g_o)
        d = jnp.where(ok, mm(u, stack_heads(e), NT), 0.0).astype(BF16)
        dq = mm(d, stack_heads(k)) + mm(u, stk[s, p], NT)
        d_t = jnp.where(ok_t, mm(e, us, NT), 0.0).astype(BF16)
        dk = mm(d_t, qs) + mm(e, gk_low[s, p])
        b_t = jnp.where(ok_t, mm(e, ws, NT), 0.0).astype(BF16)
        dv = mm(b_t, gos) + mm(e, gv_low[s, p])
        a_t = jnp.where(ok_t, mm(k, qs, NT), 0.0).astype(BF16)
        g_t = jnp.where(ok_t, mm(v, gos, NT), 0.0).astype(BF16)
        de = mm(a_t, us) + mm(g_t, ws) + dz_sum[s, p] + mm(v, gv_low[s, p], NT) + mm(k, gk_low[s, p], NT)
        proj_low[rows(s), p * 128 : (p + 1) * 128] = dq.astype(BF16)
        proj_low[rows(s), D + p * 128 : D + (p + 1) * 128] = dk.astype(BF16)
        proj_low[rows(s), 2 * D + p * 128 : 2 * D + (p + 1) * 128] = dv.astype(BF16)
        proj_low[rows(s), 3 * D + p * 128 : 3 * D + (p + 1) * 128] = (de * e.astype(F32)).astype(BF16)


WIN_R = 64


def attn_back_kernel(layer, carried, *refs):
    ids, x, qkve, att, stk, stv, do, gmid, vec, wi_m, wi_o = refs[:11]
    gh_out, proj_low, gk_out, gv_out, gz_out, small, wi_v, gk, gv, gz, sems = refs[-11:]
    first = pl.program_id(0) == 0

    @pl.when(first)
    def _():
        start_weight(ids[0] == layer, wi_m, wi_o, wi_v, sems.at[0])
        if carried:
            gk_in, gv_in, gz_in, small_in = refs[11:15]
            gk[...], gv[...], gz[...], small[...] = gk_in[...], gv_in[...], gz_in[...], small_in[...]
        else:
            for ref in (small, gk, gv, gz):
                ref[...] = jnp.zeros_like(ref)

    attend_back_block(qkve, att, stk, stv, do, proj_low, gk, gv, gz)

    @pl.when(first)
    def _():
        wait_weight(wi_m, wi_v, sems.at[0])

    g1 = mm(proj_low[...], wi_v[...], NT)
    h = x[...].astype(BF16).astype(F32)
    xh, r = hat(h)
    small[V_GAIN1 : V_GAIN1 + 1, :] += jnp.sum(g1 * xh, axis=0, keepdims=True)
    small[V_BIAS1 : V_BIAS1 + 1, :] += jnp.sum(g1, axis=0, keepdims=True)
    gh = gmid[...] + norm_back(g1 * vec[V_GAIN1 : V_GAIN1 + 1, :], xh, r)
    gh_out[...] = gh.astype(gh_out.dtype)
    gk_out[...], gv_out[...], gz_out[...] = gk[...], gv[...], gz[...]


def run_attn_back(layer, top, steps, carry, ids, x, qkve, att, stk, stv, do, gmid, vec, weight, deps=()):
    def back(width):
        return pl.BlockSpec((ROWS, width), lambda c, ids: (top - 1 - c, 0))

    if layer == 0:
        x_spec = pl.BlockSpec((ROWS, D), lambda c, ids: (ids[0] * STEPS + top - 1 - c, 0))
    else:
        x_spec = back(D)
    state = pl.BlockSpec((SUBS, PAIRS, 128, 128), lambda c, ids: (top - 1 - c, 0, 0, 0))
    carry_shapes = [(PAIRS, 128, 128), (PAIRS, 128, 128), (1, D), (VROWS, D)]
    in_specs = [x_spec, back(4 * D), pl.BlockSpec((3, ROWS, D), lambda c, ids: (0, top - 1 - c, 0)),
                state, state, back(D), back(D), const_block((VROWS, D)), ANY, ANY]
    operands = [x, qkve, att, stk, stv, do, gmid, vec, *weight]
    aliases = {}
    if carry is not None:
        gh, proj, *small_carry = carry
        in_specs = in_specs + [const_block(shape) for shape in carry_shapes] + [ANY, ANY]
        operands = operands + small_carry + [gh, proj]
        aliases = {len(operands) - 1: 0, len(operands): 1}
    return call(
        functools.partial(attn_back_kernel, layer, carry is not None), (ids,), (steps,), operands,
        in_specs,
        [back(D), back(4 * D)] + [const_block(shape) for shape in carry_shapes],
        [pltpu.VMEM((D, 4 * D), BF16)] + attention_scratch()[:3] + [pltpu.SemaphoreType.DMA((1,))],
        [
            jax.ShapeDtypeStruct((LEN, D), F32 if layer == 0 else BF16),
            jax.ShapeDtypeStruct((LEN, 4 * D), BF16),
        ] + [jax.ShapeDtypeStruct(shape, F32) for shape in carry_shapes],
        f"backward_attention{layer}", 9e9 * steps / STEPS, 17e6 * steps / STEPS, deps, aliases)


def in_grad_kernel(ids, n1, proj, keep, send):
    sec, code = ids[0], ids[1]
    for t, dst in ((1, send), (0, keep)):
        half = jnp.where(sec == t, 0, 1)
        n1h = n1[:, pl.ds(pl.multiple_of(half * 256, 256), 256)]
        acc = mm(n1h, proj[...], TN)
        for j in range(16):
            spot = position(j ^ code, half)
            for cg in range(4):
                dst[spot, cg * 16 : (cg + 1) * 16, :] = acc[j * 16 : (j + 1) * 16, cg * 512 : (cg + 1) * 512].astype(BF16)


def run_in_grad(ids, n1, proj, deps=()):
    shape = (16, WIN_R, 512)
    return call(
        in_grad_kernel, (ids,), (1,), [n1, proj],
        [const_block((LEN, D)), const_block((LEN, 4 * D))],
        [const_block(shape), const_block(shape)],
        [],
        [jax.ShapeDtypeStruct(shape, BF16)] * 2,
        "in_grad", 2200000000.0, 7000000.0, deps)


def compute(ids, wseq, inputs, cot, vec0, vec1, weights, comm=None):
    step = comm.step if comm else lambda token: ()
    start = comm.start if comm else lambda *a: None

    def attn_back(layer, token, x, qkve, att, stk, stv, do, gmid, vec):
        carry, top = None, STEPS
        while top > 0:
            carry = run_attn_back(layer, top, BACK_STEPS, carry, ids, x, qkve, att, stk, stv, do, gmid, vec, weights[0],
                                  deps=step(token))
            token = carry[5]
            top -= BACK_STEPS
        return carry[0], carry[1], carry[5]

    (out0, n1, qkve, att, stk, stv, rd, mid, n2, act, dgl, mass0) = run_fwd0(ids, inputs, vec0, weights, deps=step(None))
    (out1, n1b, qkveb, attb, stkb, stvb, gmid1, do1, mass1, small1a, *f1) = run_fwd1(
        ids, wseq, out0, cot, vec1, weights, deps=step(mass0))
    start("f1", f1)
    start("outputs", out0, out1)
    gh1, proj1, small1b = attn_back(1, mass1, out0, qkveb, attb, stkb, stvb, do1, gmid1, vec1)
    a1 = run_in_grad(ids, n1b, proj1, deps=step(small1b))
    gmid0, do0, small0a, *f0 = run_ffn0(ids, gh1, mid, n2, act, dgl, rd, vec0, weights[1:], deps=step(a1[0]))
    start("mix", a1, f0)
    gh0, proj0, small0b = attn_back(0, small0a, inputs, qkve, att, stk, stv, do0, gmid0, vec0)
    a0 = run_in_grad(ids, n1, proj0)
    step(a0[0])
    start("a0", a0)
    return (out0, out1, gh0, gh1, mass0 + mass1, small0a + small0b, small1a + small1b, f0, a0, f1, a1)


class Transfers:
    def __init__(self):
        self.active, self.results = [], {}

    def start(self, name, *parts):
        if name == "outputs":
            first, second = parts
            self.results[name] = (first, to_core(first, 0), second, to_core(second, 1))
            return
        self.results[name] = []
        if name == "small":
            self.active.append([sum_small(*parts, self.results[name]), False])
            return
        core = {"0": 0, "1": 1}.get(name[-1])
        phase = sum_phase(parts, core, self.results[name])
        self.active.append([phase, False])

    def step(self, token):
        deps = []
        for entry in reversed(self.active):
            phase, begun = entry
            try:
                deps.extend(phase.send(token if begun else None))
            except StopIteration:
                pass
            entry[1] = True
        return deps

    def finish(self, work):
        ready = []
        for _ in range(12):
            made = work(self.results)
            ready = self.step(ready + ([] if made is None else [made]))


def cores_swap(x):
    return lax.ppermute(x, "section", [(0, 1), (1, 0)])


def to_core(x, core):
    return lax.ppermute(x, "section", [(1 - core, core)])


def exchange(x, axis, by):
    return lax.ppermute(x, axis, [(i, i ^ by) for i in range(lax.axis_size(axis))])


def add_low(*terms):
    total = terms[0].astype(F32)
    for term in terms[1:]:
        total = total + term.astype(F32)
    return total.astype(BF16)


def exchange_by_core(x, *by):
    dp, rep = lax.axis_size("dp"), lax.axis_size("rep")
    pairs = [
        ((s * dp + z) * rep + r, (s * dp + (z ^ by[s][1])) * rep + (r ^ by[s][0]))
        for s in range(2) for z in range(dp) for r in range(rep)
    ]
    return lax.ppermute(x, ("section", "dp", "rep"), pairs)


FIRST = ((1, 0), (2, 0))
SECOND = ((2, 0), (0, 1))
THIRD = ((0, 1), (1, 0))


def after(token, *arrays):
    tokens = token if isinstance(token, list) else [] if token is None else [token]
    if not tokens:
        return arrays
    return lax.optimization_barrier((*arrays, *tokens))[: len(arrays)]


def sum_phase(parts, core, result):
    keep = parts[0][0] if len(parts) == 1 else jnp.concatenate([k for k, _ in parts], axis=1)
    send = parts[0][1] if len(parts) == 1 else jnp.concatenate([s for _, s in parts], axis=1)
    got = cores_swap(send)
    token = yield [keep]
    (got,) = after(token, got)
    away, home = add_low(keep[8:], got[8:]), add_low(keep[:8], got[:8])
    got = exchange_by_core(away, *FIRST)
    token = yield [away, home]
    (got,) = after(token, got)
    away, home = add_low(home[4:], got[4:]), add_low(home[:4], got[:4])
    got = exchange_by_core(away, *SECOND)
    token = yield [away, home]
    (got,) = after(token, got)
    home, got = (x.reshape(2, 2, *x.shape[1:]) for x in (home, got))
    away, home = add_low(home[:, 1], got[:, 1]), add_low(home[:, 0], got[:, 0])
    got = exchange_by_core(away, *THIRD)
    token = yield [away, home]
    (got,) = after(token, got)
    away, home = add_low(home[1], got[1]), add_low(home[0], got[0])
    got = exchange(away, "dp", 2)
    token = yield [away, home]
    (got,) = after(token, got)
    s = add_low(home, got)
    bit = 4
    while bit < lax.axis_size("dp"):
        s = add_low(s, exchange(s, "dp", bit))
        bit *= 2
    got = exchange(s, "dp", 2)
    token = yield [s]
    (got,) = after(token, got)
    s = jnp.stack([s, got])
    got = exchange_by_core(s, *THIRD)
    token = yield [s]
    (got,) = after(token, got)
    s = jnp.stack([s, got], axis=1).reshape(4, *s.shape[1:])
    got = exchange_by_core(s, *SECOND)
    token = yield [s]
    (got,) = after(token, got)
    low = jnp.concatenate([s, got], axis=0)
    high = exchange_by_core(low, *FIRST)
    send_on = cores_swap if core is None else lambda x: to_core(x, core)
    far_low = send_on(low)
    token = yield [low]
    (high,) = after(token, high)
    result.extend([low, high, far_low, send_on(high)])
    yield [high]


def sum_small(x, result):
    for axis in ("section", "rep", "dp"):
        bit = 1
        while bit < lax.axis_size(axis):
            got = exchange(x, axis, bit)
            token = yield [x]
            (got,) = after(token, got)
            x = x + got
            bit *= 2
    result.append(x)
    yield [x]


def pick_source(ids, h, own0, recv0, own1, recv1, body):
    layer_one = ids[0] == 1
    own_half = h == ids[0]
    for src, use in (
        (own0, jnp.logical_and(jnp.logical_not(layer_one), own_half)),
        (recv0, jnp.logical_and(jnp.logical_not(layer_one), jnp.logical_not(own_half))),
        (own1, jnp.logical_and(layer_one, own_half)),
        (recv1, jnp.logical_and(layer_one, jnp.logical_not(own_half))),
    ):
        @pl.when(use)
        def _(src=src):
            body(src)


def source_specs(shape, inner):
    rest = (0,) * (len(shape) - 1)

    def spec(layer, own):
        def index(h, i, ids):
            used = jnp.logical_and(ids[0] == layer, (h == ids[0]) == own)
            return (jnp.where(used, inner(i, ids), 0),) + rest

        return pl.BlockSpec(shape, index)

    return [spec(0, True), spec(0, False), spec(1, True), spec(1, False)]


def unpack_kernel(store, offsets, ids, *refs):
    sources, outs, (buf, sems) = refs[:8], refs[8:-2], refs[-2:]
    sec, code = ids[0], ids[1]
    h = pl.program_id(0)

    def fetch(half, slot, start):
        for k, part in enumerate(sources):
            layer, received, upper = k // 4, (k // 2) % 2, k % 2
            def copy(part=part, upper=upper, layer=layer):
                src = part.at[:, pl.ds(offsets[layer], buf.shape[2]), :]
                return pltpu.make_async_copy(src, buf.at[slot, pl.ds(8 * upper, 8)], sems.at[slot, upper])

            if start:
                @pl.when(jnp.logical_and(sec == layer, (half == sec) == (received == 0)))
                def _(copy=copy):
                    copy().start()
            elif k < 2:
                copy().wait()

    @pl.when(h == 0)
    def _():
        fetch(0, 0, True)
        fetch(1, 1, True)

    fetch(h, h, False)
    for j in range(16):
        store(j, buf.at[h, position(j ^ code, h)], outs)


def store_ffn(j, src, outs):
    up, out, down = outs
    for cg in range(4):
        up[j * 16 : (j + 1) * 16, cg * 512 : (cg + 1) * 512] = src[cg * 16 : (cg + 1) * 16, :].astype(F32)
    out[j * 16 : (j + 1) * 16, :] = src[64:80, :].astype(F32)
    down[j * 64 : (j + 1) * 64, :] = src[80:144, :].astype(F32)


def store_in(j, src, outs):
    for cg in range(4):
        outs[0][j * 16 : (j + 1) * 16, cg * 512 : (cg + 1) * 512] = src[cg * 16 : (cg + 1) * 16, :].astype(F32)


def unpack(ids, sources, store, shapes, rows, offsets, name, deps=()):
    return call(
        functools.partial(unpack_kernel, store, offsets), (ids,), (2,), sources,
        [ANY] * 8,
        [pl.BlockSpec((shape[0] // 2, shape[1]), lambda h, ids: (h, 0)) for shape in shapes],
        [pltpu.VMEM((2, 16, rows, 512), BF16), pltpu.SemaphoreType.DMA((2, 2))],
        [jax.ShapeDtypeStruct(shape, F32) for shape in shapes],
        name, 1000000.0, 3 * 4 * 8192 * rows, deps)


def assemble_kernel(ids, own0, recv0, own1, recv1, out):
    def body(src):
        out[...] = src[...].astype(F32)

    pick_source(ids, pl.program_id(0), own0, recv0, own1, recv1, body)


def assemble(ids, sources, name, deps=()):
    return call(
        assemble_kernel, (ids,), (2, 2), sources,
        source_specs((512, D), lambda i, ids: i),
        [pl.BlockSpec((512, D), lambda h, i, ids: (h * 2 + i, 0))],
        [],
        [jax.ShapeDtypeStruct((2 * LEN, D), F32)],
        name, 1000000.0, 8000000.0, deps)[0]


def pack_vectors(norm_gains, norm_biases, in_bias, out_bias):
    rows = [norm_gains[0], norm_biases[0], out_bias, in_bias.reshape(4, D)]
    used = sum(r.shape[0] for r in rows)
    return jnp.concatenate(rows + [jnp.zeros((VROWS - used, D), BF16)], axis=0)


def per_device(inputs, cotangent, domain_ids, group_of, group_weights, norm_gains, norm_biases,
               w_in, w_out, w_up, in_bias, w_down, out_bias):
    sec = lax.axis_index("section")
    code = lax.axis_index("rep") * 4 + lax.axis_index("dp") % 4
    ids = jnp.stack([sec, code]).astype(jnp.int32)
    leading = sec == 0
    mine = [w_in[0], w_out[0], w_up[0], w_down[0]]
    vec_mine = pack_vectors(norm_gains, norm_biases, in_bias, out_bias)
    vec_other = cores_swap(vec_mine)
    weights = [(w, cores_swap(w)) for w in mine]
    vec0 = jnp.where(leading, vec_mine, vec_other).astype(F32)
    vec1 = jnp.where(leading, vec_other, vec_mine).astype(F32)
    own_id = jnp.where(leading, domain_ids[0], domain_ids[1])
    domain_hit = own_id == jnp.arange(group_of.shape[0])
    group = jnp.sum(jnp.where(domain_hit, group_of, 0))
    wseq = jnp.sum(jnp.where(group == jnp.arange(group_weights.shape[0]), group_weights, 0.0)).reshape(1)

    comm = Transfers()
    (out0, out1, gh0, gh1, mass, small0, small1, *_) = compute(ids, wseq, inputs, cotangent, vec0, vec1, weights, comm)
    made = {}
    comm.results["grads"] = (gh0, to_core(gh0, 0), gh1, to_core(gh1, 1))

    def work(got):
        if "outputs" not in made:
            made["outputs"] = assemble(ids, got["outputs"], "layer_outputs")
            return made["outputs"]
        if "grads" not in made:
            made["grads"] = assemble(ids, got["grads"], "input_grads")
            return made["grads"]
        if "ffn" not in made and got["mix"] and got["f1"]:
            shapes = ((D, FF), (D, D), (FF, D))
            made["ffn"] = unpack(ids, got["mix"] + got["f1"], store_ffn, shapes, FFN_R, (WIN_R, 0), "unpack_ffn")
            return made["ffn"][0]
        return None

    comm.start("small", jnp.concatenate([small0[:9], small1[:9], mass, jnp.zeros((5, D), F32)], axis=0))
    comm.finish(work)
    got = comm.results
    layer_outputs, input_grads = made["outputs"], made["grads"]
    g_up, g_wout, g_down = made["ffn"]
    (g_win,) = unpack(ids, got["a0"] + got["mix"], store_in, ((D, 4 * D),), WIN_R, (0, 0), "unpack_in")

    (total,) = got["small"]
    small = jnp.where(leading, total[:9], total[9:18])
    slot_mass = jnp.sum(total[18].reshape(HEADS, SLOTS), axis=0) / (HEADS * 2 * LEN)
    return (
        layer_outputs[None],
        input_grads[None],
        small[0:2][None],
        small[2:4][None],
        g_win[None],
        g_wout[None],
        g_up[None],
        small[V_INB : V_INB + 4].reshape(1, FF),
        g_down[None],
        small[V_OUTB][None],
        slot_mass,
    )


def solution(mesh):
    return jax.shard_map(
        per_device,
        mesh=mesh,
        in_specs=(
            P(("dp", "rep"), None),
            P(("dp", "rep"), None),
            P(("dp", "rep")),
            P(),
            P(),
            P("section", None, None),
            P("section", None, None),
            P("section", None, None),
            P("section", None, None),
            P("section", None, None),
            P("section", None),
            P("section", None, None),
            P("section", None),
        ),
        out_specs=(
            P("section", ("dp", "rep"), None),
            P("section", ("dp", "rep"), None),
            P("section", None, None),
            P("section", None, None),
            P("section", None, None),
            P("section", None, None),
            P("section", None, None),
            P("section", None),
            P("section", None, None),
            P("section", None),
            P(),
        ),
        check_vma=False,
    )
```
